512 devices in a mesh: sec: 4 (over x), seq: 32 (over z, core), tp: 4 (over y).
Axes of the slice: x: 4, y: 4, z: 16, core: 2. Of those that a mesh axis runs over, the one named last changes fastest.
Arguments:
- text_embed: bfloat16 [32768, 8192], P(('sec', 'seq'), 'tp'), may hold values from -6 to 6
- image_rows: bfloat16 [16384, 8192], P(('sec', 'seq'), 'tp'), may hold values from -6 to 6
- token_source: int32 [32768], P(('sec', 'seq')), may hold values from -1 to 16383, as said below
- slot_dest: int32 [16384], P(('sec', 'seq')), may hold values from -1 to 32767, as said below
- norm_gain: float32 [8192], P('tp'), may hold values from 0.1 to 1.9
- kv_weight: bfloat16 [1024, 8192], P(('sec', 'seq'), 'tp'), may hold values from -0.0625 to 0.0625
- kv_cot: bfloat16 [32768, 1024], P(('sec', 'seq'), 'tp'), may hold values from -6 to 6
Outputs:
- key_value: bfloat16 [32768, 1024], P(('sec', 'seq'), 'tp')
- text_grad: bfloat16 [32768, 8192], P(('sec', 'seq'), 'tp')
- image_grads: bfloat16 [16384, 8192], P(('sec', 'seq'), 'tp')
The draws below stay inside these ranges and needn't reach their ends.
Inputs may be any that keep to these rules, and one draw needn't show every extreme that they name: Encoder device e's slot s has index e * 128 + s; token_source and slot_dest are inverse to each other. The slots of one encoder device that fill tokens of one device's 256 tokens stand in the order of those tokens, at most 2 of them, and in every draw some encoder device fills exactly 2 tokens of some device. `slot_dest`: the inverse of token_source.
All inputs are finite; a program needn't handle non-finite values.
Results may differ from the reference program's by a relative error of at most 0.0049.
Values may be sent and summed in bfloat16 or wider, within the bound.
A program may use at most 64 MiB of HBM per device.

```python
import jax
import jax.numpy as jnp
from jax import lax

D = 8192
KVW = 512
TOK_DEV = 256
N_ENC = 128
ENC_SLOTS = 128
TOKENS = 32768
N_SEC = 4
N_SEQ = 32


def layout_source(key):
    first_key, second_key, third_key = jax.random.split(jax.random.fold_in(key, 11), 3)
    enc_count = N_SEC * N_SEQ
    unit_len = TOK_DEV // 8
    pair_count = TOKENS // (2 * unit_len)
    pair_kind = jax.random.randint(first_key, (pair_count,), 0, 4)
    first_img = (pair_kind == 1) | (pair_kind == 3)
    second_img = pair_kind == 2
    unit_img = jnp.stack([first_img, second_img], axis=1).reshape(-1)
    shard_of_unit = jnp.arange(2 * pair_count, dtype=jnp.int32) // 8
    forced = jax.random.randint(second_key, (), 0, N_SEQ).astype(jnp.int32)
    partner = jnp.bitwise_xor(forced, 1)
    unit_img = jnp.where(shard_of_unit == forced, True, jnp.where(shard_of_unit == partner, False, unit_img))
    token_img = jnp.repeat(unit_img, unit_len).astype(jnp.int32)
    row_order = jnp.cumsum(token_img) - token_img
    rotation = jax.random.randint(third_key, (), 0, enc_count).astype(jnp.int32)
    encoder = (row_order + rotation) % enc_count
    slot_index = row_order // enc_count
    return jnp.where(token_img > 0, encoder * ENC_SLOTS + slot_index, -1).astype(jnp.int32)


def draw_token_source(key, part):
    return layout_source(key)


def draw_slot_dest(key, part):
    source = layout_source(key)
    total_slots = N_SEC * N_SEQ * ENC_SLOTS
    target = jnp.where(source >= 0, source, total_slots)
    empty = jnp.full((total_slots,), -1, jnp.int32)
    return empty.at[target].set(jnp.arange(TOKENS, dtype=jnp.int32), mode='drop')


def block_levels(stream_key, shape, shards, least, top_value):
    def one(position, parts):
        draws = jax.random.uniform(jax.random.fold_in(jax.random.fold_in(stream_key, 6), position), (parts,), jnp.float32, least / len(shards), top_value / len(shards))
        return jnp.repeat(jnp.exp(draws), shape[position] // parts).reshape((-1,) + (1,) * (len(shape) - position - 1))

    level = one(*shards[0])
    for cut in shards[1:]:
        level = level * one(*cut)
    return level


def gaussian(rng, dims, spread, limit, cuts=(), kind=jnp.bfloat16):
    factor_of = block_levels(rng, dims, cuts, -0.22, 0.18) if cuts else 1.0
    entries = jax.random.normal(rng, dims, jnp.float32) * spread * factor_of
    return jnp.minimum(jnp.maximum(entries, -limit), limit).astype(kind)


def setup_inputs(seed: int = 0) -> dict:
    key_of = jax.random.split(jax.random.key(seed), 8)
    return {
        "text_embed": gaussian(key_of[0], (TOKENS, D), 1.0, 6.0, ((0, 128), (1, 4))),
        "image_rows": gaussian(key_of[1], (N_ENC * ENC_SLOTS, D), 1.0, 6.0, ((0, 128), (1, 4))),
        "token_source": draw_token_source(jax.random.fold_in(key_of[7], 71), 0),
        "slot_dest": draw_slot_dest(jax.random.fold_in(key_of[7], 71), 0),
        "norm_gain": jnp.clip(1.0 + 0.18 * jax.random.normal(key_of[4], (D,), jnp.float32), 0.1, 1.9),
        "kv_weight": gaussian(key_of[5], (2 * KVW, D), D ** -0.5, 0.0625, ((0, 128), (1, 4))),
        "kv_cot": gaussian(key_of[6], (TOKENS, 2 * KVW), 1.0, 6.0, ((0, 128), (1, 4))),
    }


epsilon = 1e-06

def reference(text_embed, image_rows, token_source, slot_dest, norm_gain, kv_weight, kv_cot):
    is_image = token_source >= 0
    picked = jnp.take(image_rows, jnp.where(is_image, token_source, 0).astype(jnp.int32), axis=0)
    mixed = jnp.where(is_image[:, None], picked, text_embed)
    gain = norm_gain.astype(jnp.float32)

    def block(inputs):
        rows, cot_rows = inputs
        hidden = rows.astype(jnp.float32)
        scale = lax.rsqrt(lax.optimization_barrier(jnp.sum(hidden * hidden, axis=1)) / D + epsilon)
        normed = (hidden * scale[:, None] * gain).astype(jnp.bfloat16)
        key_value = lax.dot_general(normed, kv_weight, (((1,), (1,)), ((), ())), preferred_element_type=jnp.float32).astype(jnp.bfloat16)
        normed_grad = jnp.dot(cot_rows, kv_weight, preferred_element_type=jnp.float32)
        scaled_grad = gain * normed_grad
        dots = lax.optimization_barrier(jnp.sum(scaled_grad * hidden, axis=1))
        input_grad = scale[:, None] * scaled_grad - hidden * (scale * scale * scale * dots / D)[:, None]
        return (key_value, input_grad.astype(jnp.bfloat16))
    blocks = TOKENS // TOK_DEV
    key_value, input_grad = lax.map(block, (mixed.reshape(blocks, TOK_DEV, D), kv_cot.reshape(blocks, TOK_DEV, 2 * KVW)))
    key_value = key_value.reshape(TOKENS, 2 * KVW)
    input_grad = input_grad.reshape(TOKENS, D)
    text_grad = jnp.where(is_image[:, None], jnp.zeros_like(input_grad), input_grad)
    filled = slot_dest >= 0
    image_grads = jnp.take(input_grad, jnp.where(filled, slot_dest, 0).astype(jnp.int32), axis=0)
    image_grads = jnp.where(filled[:, None], image_grads, jnp.zeros_like(image_grads))
    return (key_value, text_grad, image_grads)
```

```python
import jax
import jax.numpy as jnp
from jax import lax
from jax.sharding import PartitionSpec as P

D = 8192
EPS = 1e-06


def pair_position(owner):
    n = owner.shape[0]
    order = jnp.arange(n, dtype=jnp.int32)
    same = (owner[:, None] == owner[None, :]) & (order[:, None] < order[None, :])
    rank = jnp.sum(same.astype(jnp.int32), axis=0)
    return jnp.where(owner >= 0, 2 * owner + rank, -1)


def per_device(text_embed, image_rows, token_source, slot_dest, norm_gain, kv_weight, kv_cot):
    tok = text_embed.shape[0]
    slots = image_rows.shape[0]
    axes = ("sec", "seq")
    peers = lax.axis_size("sec") * lax.axis_size("seq")
    place = jnp.arange(2 * peers, dtype=jnp.int32)
    is_image = token_source >= 0
    filled = slot_dest >= 0
    pos_tok = pair_position(jnp.where(is_image, token_source // slots, -1))
    pos_slot = pair_position(jnp.where(filled, slot_dest // tok, -1))
    pick_tok = (place[:, None] == pos_tok[None, :]).astype(jnp.bfloat16)
    pick_slot = (place[:, None] == pos_slot[None, :]).astype(jnp.bfloat16)

    def move(pick_send, pick_recv, rows):
        send = jnp.dot(pick_send, rows, preferred_element_type=jnp.float32).astype(jnp.bfloat16)
        got = lax.all_to_all(send, axes, split_axis=0, concat_axis=0, tiled=True)
        return lax.dot_general(
            pick_recv, got, (((0,), (0,)), ((), ())), preferred_element_type=jnp.float32
        ).astype(jnp.bfloat16)

    cot_img = move(pick_tok, pick_slot, kv_cot)
    cot = lax.all_gather(jnp.concatenate([kv_cot, cot_img]), "tp", axis=1, tiled=True)
    weight = lax.all_gather(kv_weight, axes, axis=0, tiled=True)
    rows = jnp.concatenate([text_embed, image_rows]).astype(jnp.float32)
    gained = (rows * norm_gain).astype(jnp.bfloat16)
    partial = lax.dot_general(
        gained, weight, (((1,), (1,)), ((), ())), preferred_element_type=jnp.float32
    )
    sums = jnp.stack([jnp.sum(rows * rows, axis=1), jnp.sum(partial * cot.astype(jnp.float32), axis=1)])
    sumsq, dots = lax.psum(sums, "tp")
    scale = lax.rsqrt(sumsq / D + EPS)
    raw = lax.psum_scatter(partial, "tp", scatter_dimension=1, tiled=True)
    kv = (raw * scale[:, None]).astype(jnp.bfloat16)
    kv_img = move(pick_slot, pick_tok, kv[tok:])
    key_value = jnp.where(is_image[:, None], kv_img, kv[:tok])
    normed_grad = jnp.dot(cot, weight, preferred_element_type=jnp.float32)
    grad = scale[:, None] * (norm_gain * normed_grad) - rows * (scale * scale * scale * dots / D)[:, None]
    grad = grad.astype(jnp.bfloat16)
    text_grad = jnp.where(is_image[:, None], jnp.zeros_like(grad[:tok]), grad[:tok])
    image_grads = jnp.where(filled[:, None], grad[tok:], jnp.zeros_like(grad[tok:]))
    return key_value, text_grad, image_grads


def solution(mesh):
    both = P(("sec", "seq"), "tp")
    rows = P(("sec", "seq"))
    return jax.shard_map(
        per_device,
        mesh=mesh,
        in_specs=(both, both, rows, rows, P("tp"), both, both),
        out_specs=(both, both, both),
        check_vma=False,
    )
```

```python
import functools

import jax
import jax.numpy as jnp
from jax import lax
from jax.experimental import pallas as pl
from jax.experimental.pallas import tpu as pltpu
from jax.sharding import PartitionSpec as P

D = 8192
EPS = 1e-06
F32 = jnp.float32
BF16 = jnp.bfloat16
MESH = pl.DeviceIdType.MESH
LANES = 128


class Pair:
    def __init__(self, out, into):
        self.ends = (out, into)

    def __getitem__(self, i):
        return self.ends[i]()


def shift_of(n):
    return n.bit_length() - 1


def places(row, log_owner, nx, nseq):
    n = row.shape[1]
    own = lax.shift_right_arithmetic(row, jnp.full_like(row, log_owner))
    own_row = own.astype(F32)
    ii = lax.broadcasted_iota(jnp.int32, (n, n), 0)
    jj = lax.broadcasted_iota(jnp.int32, (n, n), 1)
    own_col = jnp.sum(jnp.where(ii == jj, own_row, 0.0), axis=1, keepdims=True)
    eq = own_col == own_row
    rank_row = jnp.sum(jnp.where(eq & (ii < jj), 1.0, 0.0), axis=0, keepdims=True)
    rank_col = jnp.sum(jnp.where(eq & (jj < ii), 1.0, 0.0), axis=1, keepdims=True)
    x_of = lax.shift_right_arithmetic(own, jnp.full_like(own, shift_of(nseq)))
    s_of = own & (nseq - 1)
    key = ((s_of * nx + x_of) * 2).astype(F32) + rank_row
    key = jnp.where(own_row >= 0.0, key, -1.0)
    pos = jnp.where(own_col >= 0.0, own_col * 2.0 + rank_col, -1.0)
    return key, pos, own_col


def kernel(
    nx, nz, ny,
    text, img, ts, sd, gain, w, cot,
    kv_out, tg_out, ig_out,
    wsend, wsib, wq, xg, cots, sq, acc, kvp, rs_send, rs_recv, sum_send, sum_recv,
    b1a, r1a, b2a, r2a, b1b, r1b, b2b, r2b,
    sib_sem, ax_s, ax_r, z_s, z_r, bx_s, bx_r, sa_s, sa_r, sb_s, sb_r,
    e1_s, e1_r, e2_s, e2_r, yc_s, yc_r, rs_s, rs_r, sm_s, sm_r,
):
    x, s, y = lax.axis_index("sec"), lax.axis_index("seq"), lax.axis_index("tp")
    z, c = s // 2, s % 2
    nseq = 2 * nz
    tok, feat = text.shape
    slots = img.shape[0]
    rows = tok + slots
    cols = cot.shape[1]
    halves = cols // LANES
    npos = 2 * nx * nseq
    fq = feat // 4
    nr, nl = nz // 2, (nz - 1) // 2

    def remote(src, dst, ss, rs, dev):
        return pltpu.make_async_remote_copy(
            src_ref=src, dst_ref=dst, send_sem=ss, recv_sem=rs, device_id=dev, device_id_type=MESH
        )

    def loop(lo, hi, body):
        if hi > lo:
            lax.fori_loop(lo, hi, lambda i, t: (body(i), t)[1], 0)

    barrier = pltpu.get_barrier_semaphore()

    def greet(dev):
        pl.semaphore_signal(barrier, inc=1, device_id=dev, device_id_type=MESH)

    loop(1, nseq, lambda k: greet((x, lax.rem(s + k, nseq), y)))
    for k in range(1, nx):
        greet((lax.rem(x + k, nx), s, y))
    for k in range(1, ny):
        greet((x, s, lax.rem(y + k, ny)))

    half = feat // 2
    w8 = w[...].astype(F32)
    wsend[...] = jnp.concatenate([w8[:, :half], w8[:, half:]], axis=0).astype(BF16)
    key_tok, pos_tok, own_tok = places(ts[...], shift_of(slots), nx, nseq)
    key_slot, pos_slot, own_slot = places(sd[...], shift_of(tok), nx, nseq)

    def pick_rows(key):
        n = key.shape[1]
        return jnp.where(lax.broadcasted_iota(jnp.int32, (npos, n), 0).astype(F32) == key, 1.0, 0.0).astype(BF16)

    def pick_cols(pos):
        n = pos.shape[0]
        return jnp.where(lax.broadcasted_iota(jnp.int32, (n, npos), 1).astype(F32) == pos, 1.0, 0.0).astype(BF16)

    def fill1(key, values, b1, r1):
        g = jnp.dot(pick_rows(key), values, preferred_element_type=F32)
        parts = [g[:, h * LANES : (h + 1) * LANES].reshape(nseq, 2 * nx, LANES) for h in range(halves)]
        b1[...] = jnp.concatenate(parts, axis=1).astype(BF16)
        r1[s] = b1[s]

    def fill2(r1, b2, r2):
        r = r1[...].astype(F32)
        m = jnp.concatenate(
            [r[:, h * 2 * nx : (h + 1) * 2 * nx].reshape(npos, LANES) for h in range(halves)], axis=1
        ).astype(BF16)
        i = lax.broadcasted_iota(jnp.int32, (npos, npos), 0)
        j = lax.broadcasted_iota(jnp.int32, (npos, npos), 1)
        lx, ls = shift_of(2 * nseq), shift_of(nseq)
        i_x = lax.shift_right_arithmetic(i, jnp.full_like(i, lx))
        i_s = lax.shift_right_arithmetic(i, jnp.full_like(i, 1)) & (nseq - 1)
        perm = jnp.where((i_s * nx + i_x) * 2 + (i & 1) == j, 1.0, 0.0).astype(BF16)
        b2[...] = jnp.dot(perm, m, preferred_element_type=F32).astype(BF16).reshape(nx, 2 * nseq, cols)
        r2[x] = b2[x]

    def take(pos, r2):
        return jnp.dot(pick_cols(pos), r2[...].reshape(npos, cols), preferred_element_type=F32)

    def copy1(n, b1, r1, k):
        to, frm = lax.rem(s + k, nseq), lax.rem(s + nseq - k, nseq)
        return Pair(
            lambda: remote(b1.at[to], r1.at[s], e1_s.at[n, k], e1_r.at[n, k], (x, to, y)),
            lambda: remote(b1.at[to], r1.at[frm], e1_s.at[n, k], e1_r.at[n, k], (x, to, y)),
        )

    def copy2(n, b2, r2, k):
        to, frm = lax.rem(x + k, nx), lax.rem(x + nx - k, nx)
        return Pair(
            lambda: remote(b2.at[to], r2.at[x], e2_s.at[n, k], e2_r.at[n, k], (to, s, y)),
            lambda: remote(b2.at[to], r2.at[frm], e2_s.at[n, k], e2_r.at[n, k], (to, s, y)),
        )

    fill1(key_tok, cot[...], b1a, r1a)
    cots[y, :tok] = cot[...]

    pl.semaphore_wait(barrier, nseq - 1 + nx - 1 + ny - 1)

    sib = (x, s + 1 - 2 * c, y)
    swap = remote(wsend, wsib, sib_sem.at[0], sib_sem.at[1], sib)
    swap.start()
    loop(1, nseq, lambda k: copy1(0, b1a, r1a, k)[0].start())

    def copy_y(part, k):
        to, frm = lax.rem(y + k, ny), lax.rem(y + ny - k, ny)
        n = tok if part == 0 else slots
        lo = 0 if part == 0 else tok
        return Pair(
            lambda: remote(cots.at[y, pl.ds(lo, n)], cots.at[y, pl.ds(lo, n)], yc_s.at[part, k], yc_r.at[part, k], (x, s, to)),
            lambda: remote(cots.at[y, pl.ds(lo, n)], cots.at[frm, pl.ds(lo, n)], yc_s.at[part, k], yc_r.at[part, k], (x, s, to)),
        )

    for k in range(1, ny):
        copy_y(0, k)[0].start()

    swap.wait()
    first = c == 0
    mine = jnp.where(first, wsend[0:8].astype(F32), wsend[8:16].astype(F32))
    other = jnp.where(first, wsib[0:8].astype(F32), wsib[8:16].astype(F32))
    piece = jnp.concatenate([jnp.where(first, mine, other), jnp.where(first, other, mine)], axis=0).astype(BF16)
    qa, qb = 2 * c, 2 * c + 1
    wq[qa, x, z] = piece[:, :fq]
    wq[qb, x, z] = piece[:, fq:]

    def copy_ax(k):
        to, frm = lax.rem(x + k, nx), lax.rem(x + nx - k, nx)
        return Pair(
            lambda: remote(wq.at[qa, x, z], wq.at[qa, x, z], ax_s.at[k], ax_r.at[k], (to, s, y)),
            lambda: remote(wq.at[qa, x, z], wq.at[qa, frm, z], ax_s.at[k], ax_r.at[k], (to, s, y)),
        )

    def origin(d, k):
        return lax.rem(z + nz - k, nz) if d == 0 else lax.rem(z + k, nz)

    def block(b, o):
        return wq.at[qb, x, o] if b else wq.at[qa, :, o]

    def copy_z(b, d, k):
        to = lax.rem(z + 1, nz) if d == 0 else lax.rem(z + nz - 1, nz)
        out, into = block(b, origin(d, k - 1)), block(b, origin(d, k))
        dev = (x, 2 * to + c, y)
        return Pair(
            lambda: remote(out, out, z_s.at[b, d, k], z_r.at[b, d, k], dev),
            lambda: remote(into, into, z_s.at[b, d, k], z_r.at[b, d, k], dev),
        )

    def copy_bx(o, j, k):
        to, frm = lax.rem(x + k, nx), lax.rem(x + nx - k, nx)
        return Pair(
            lambda: remote(wq.at[qb, x, o], wq.at[qb, x, o], bx_s.at[j, k], bx_r.at[j, k], (to, s, y)),
            lambda: remote(wq.at[qb, x, o], wq.at[qb, frm, o], bx_s.at[j, k], bx_r.at[j, k], (to, s, y)),
        )

    def copy_sib(b, o, j):
        q, other_q = (qb, 3 - qa) if b else (qa, 2 - qa)
        ss, rr = (sb_s, sb_r) if b else (sa_s, sa_r)
        return Pair(
            lambda: remote(wq.at[q, :, o], wq.at[q, :, o], ss.at[j], rr.at[j], sib),
            lambda: remote(wq.at[q, :, o], wq.at[other_q, :, o], ss.at[j], rr.at[j], sib),
        )

    for k in range(1, nx):
        copy_ax(k)[0].start()
    copy_z(1, 0, 1)[0].start()
    if nl:
        copy_z(1, 1, 1)[0].start()
    for k in range(1, nx):
        copy_bx(z, 0, k)[0].start()

    def prepare(ref, base):
        def body(i):
            r = ref[pl.ds(pl.multiple_of(i * 16, 16), 16), :].astype(F32)
            at = pl.ds(pl.multiple_of(base + i * 16, 16), 16)
            xg[at, :] = (r * gain[...]).astype(BF16)
            sq[at, :] = jnp.broadcast_to(jnp.sum(r * r, axis=1, keepdims=True), (16, LANES))

        loop(0, ref.shape[0] // 16, body)

    for k in range(1, nx):
        copy_ax(k)[1].wait_recv()
    copy_z(0, 0, 1)[0].start()
    if nl:
        copy_z(0, 1, 1)[0].start()
    copy_sib(0, z, 0)[0].start()

    prepare(text, 0)

    def finish_b(o, j):
        for k in range(1, nx):
            copy_bx(o, j, k)[1].wait_recv()
        copy_sib(1, o, j)[0].start()

    def arrive(b, d, k):
        n = nr if d == 0 else nl
        o, j = origin(d, k), 2 * k - 1 + d
        copy_z(b, d, k)[1].wait_recv()

        @pl.when(k < n)
        def _():
            copy_z(b, d, k + 1)[0].start()

        if b:
            for i in range(1, nx):
                copy_bx(o, j, i)[0].start()
        else:
            copy_sib(0, o, j)[0].start()

    def ring(k):
        for b in (1, 0):
            arrive(b, 0, k)

            @pl.when(k <= nl)
            def _():
                arrive(b, 1, k)

        @pl.when(k == 1)
        def _():
            finish_b(z, 0)

        @pl.when(k > 1)
        def _():
            finish_b(origin(0, k - 1), 2 * k - 3)
            finish_b(origin(1, k - 1), 2 * k - 2)

    cut1, cut2 = max(nr // 4, 1), max(nr // 2, 1)
    loop(1, cut1 + 1, ring)
    prepare(img, tok)
    loop(1, nseq, lambda k: copy1(0, b1a, r1a, k)[1].wait_recv())
    fill2(r1a, b2a, r2a)
    for k in range(1, nx):
        copy2(0, b2a, r2a, k)[0].start()
    loop(cut1 + 1, cut2 + 1, ring)
    for k in range(1, nx):
        copy2(0, b2a, r2a, k)[1].wait_recv()
    cots[y, tok:] = take(pos_slot, r2a).astype(BF16)
    for k in range(1, ny):
        copy_y(1, k)[0].start()
    loop(cut2 + 1, nr + 1, ring)
    finish_b(origin(0, nr), 2 * nr - 1)
    if nl == nr:
        finish_b(origin(1, nr), 2 * nr)
    for part in range(2):
        for k in range(1, ny):
            copy_y(part, k)[1].wait_recv()
    for b in range(2):
        copy_sib(b, z, 0)[1].wait_recv()
        loop(1, nr + 1, lambda k, b=b: copy_sib(b, origin(0, k), 2 * k - 1)[1].wait_recv())
        loop(1, nl + 1, lambda k, b=b: copy_sib(b, origin(1, k), 2 * k)[1].wait_recv())

    def copy_rs(k):
        to = lax.rem(y + k, ny)
        return remote(rs_send.at[k], rs_recv.at[k], rs_s.at[k], rs_r.at[k], (x, s, to))

    def copy_sum(k):
        to = lax.rem(y + k, ny)
        return remote(sum_send, sum_recv.at[k], sm_s.at[k], sm_r.at[k], (x, s, to))

    dots = jnp.zeros((rows, 1), F32)
    for k in list(range(1, ny)) + [0]:
        t = lax.rem(y + k, ny)
        part = jnp.zeros((rows, cols), F32)
        for q in range(4):
            part = part + lax.dot_general(
                xg[:, q * fq : (q + 1) * fq],
                wq[q, t].reshape(16 * nz, fq),
                (((1,), (1,)), ((), ())),
                preferred_element_type=F32,
            )
        if k:
            rs_send[k] = part.astype(BF16)
            copy_rs(k).start()
        else:
            kvp[...] = part
        dots = dots + jnp.sum(part * cots[t].astype(F32), axis=1, keepdims=True)
    lane = lax.broadcasted_iota(jnp.int32, (rows, LANES), 1)
    both = jnp.where(lane == 0, sq[...], jnp.where(lane == 1, dots, 0.0))
    sum_send[...] = jnp.transpose(both)[:8]
    for k in range(1, ny):
        copy_sum(k).start()

    cot_all = jnp.concatenate([cots[t] for t in range(ny)], axis=1)
    for q in range(4):
        acc[:, q * fq : (q + 1) * fq] = jnp.dot(
            cot_all, wq[q].reshape(nx * nz * 16, fq), preferred_element_type=F32
        )

    total = sum_send[...]
    for k in range(1, ny):
        copy_sum(k).wait_recv()
        total = total + sum_recv[k]
    scale_r = lax.rsqrt(total[0:1] / D + EPS)
    coef_r = scale_r * scale_r * scale_r * total[1:2] / D
    flat = jnp.concatenate([scale_r, coef_r, jnp.zeros((LANES - 2, rows), F32)], axis=0)
    sq[...] = jnp.transpose(flat)
    scale = sq[:, 0:1]

    raw = kvp[...]
    for k in range(1, ny):
        copy_rs(k).wait_recv()
        raw = raw + rs_recv[k].astype(F32)
    kv = raw * scale
    kvp[...] = kv
    fill1(key_slot, kv[tok:].astype(BF16), b1b, r1b)
    loop(1, nseq, lambda k: copy1(1, b1b, r1b, k)[0].start())

    keep = jnp.concatenate(
        [jnp.where(own_tok < 0.0, 1.0, 0.0), jnp.where(own_slot >= 0.0, 1.0, 0.0)], axis=0
    )
    sq[...] = jnp.where(lane == 2, keep, sq[...])

    def body_of(ref, base, out):
        def body(i):
            here = pl.ds(pl.multiple_of(i * 16, 16), 16)
            at = pl.ds(pl.multiple_of(base + i * 16, 16), 16)
            r = ref[here, :].astype(F32)
            f = sq[at, :]
            g = f[:, 0:1] * (gain[...] * acc[at, :]) - r * f[:, 1:2]
            out[here, :] = jnp.where(f[:, 2:3] > 0.0, g, 0.0).astype(BF16)

        loop(0, ref.shape[0] // 16, body)

    body_of(text, 0, tg_out)
    loop(1, nseq, lambda k: copy1(1, b1b, r1b, k)[1].wait_recv())
    fill2(r1b, b2b, r2b)
    for k in range(1, nx):
        copy2(1, b2b, r2b, k)[0].start()
    body_of(img, tok, ig_out)
    for k in range(1, nx):
        copy2(1, b2b, r2b, k)[1].wait_recv()
    got = take(pos_tok, r2b)
    kv_out[...] = jnp.where(own_tok >= 0.0, got, kvp[:tok]).astype(BF16)

    for k in range(1, nx):
        copy_ax(k)[0].wait_send()
        copy_bx(z, 0, k)[0].wait_send()
        copy2(0, b2a, r2a, k)[0].wait_send()
        copy2(1, b2b, r2b, k)[0].wait_send()
    for k in range(1, ny):
        copy_y(0, k)[0].wait_send()
        copy_y(1, k)[0].wait_send()
        copy_rs(k).wait_send()
        copy_sum(k).wait_send()

    def sent1(k):
        copy1(0, b1a, r1a, k)[0].wait_send()
        copy1(1, b1b, r1b, k)[0].wait_send()

    loop(1, nseq, sent1)
    for b in range(2):
        copy_sib(b, z, 0)[0].wait_send()
        for d, n in ((0, nr), (1, nl)):

            def sent(k, b=b, d=d):
                o, j = origin(d, k), 2 * k - 1 + d
                copy_z(b, d, k)[0].wait_send()
                copy_sib(b, o, j)[0].wait_send()
                if b:
                    for i in range(1, nx):
                        copy_bx(o, j, i)[0].wait_send()

            loop(1, n + 1, sent)


def per_device(text_embed, image_rows, token_source, slot_dest, norm_gain, kv_weight, kv_cot):
    nx, nseq, ny = lax.axis_size("sec"), lax.axis_size("seq"), lax.axis_size("tp")
    nz = nseq // 2
    tok, feat = text_embed.shape
    slots = image_rows.shape[0]
    rows = tok + slots
    cols = kv_cot.shape[1]
    nr = nz // 2
    dma = pltpu.SemaphoreType.DMA
    blk = (2 * nx * cols) // LANES
    exch = [
        pltpu.VMEM((nseq, blk, LANES), BF16),
        pltpu.VMEM((nseq, blk, LANES), BF16),
        pltpu.VMEM((nx, 2 * nseq, cols), BF16),
        pltpu.VMEM((nx, 2 * nseq, cols), BF16),
    ]
    vmem = pl.BlockSpec(memory_space=pltpu.VMEM)
    return pl.pallas_call(
        functools.partial(kernel, nx, nz, ny),
        out_shape=(
            jax.ShapeDtypeStruct((tok, cols), BF16),
            jax.ShapeDtypeStruct((tok, feat), BF16),
            jax.ShapeDtypeStruct((slots, feat), BF16),
        ),
        in_specs=[vmem] * 7,
        out_specs=(vmem, vmem, vmem),
        scratch_shapes=[
            pltpu.VMEM((16, feat // 2), BF16),
            pltpu.VMEM((16, feat // 2), BF16),
            pltpu.VMEM((4, nx, nz, 16, feat // 4), BF16),
            pltpu.VMEM((rows, feat), BF16),
            pltpu.VMEM((ny, rows, cols), BF16),
            pltpu.VMEM((rows, LANES), F32),
            pltpu.VMEM((rows, feat), F32),
            pltpu.VMEM((rows, cols), F32),
            pltpu.VMEM((ny, rows, cols), BF16),
            pltpu.VMEM((ny, rows, cols), BF16),
            pltpu.VMEM((8, rows), F32),
            pltpu.VMEM((ny, 8, rows), F32),
            *exch,
            *exch,
            dma((2,)),
            dma((nx,)),
            dma((nx,)),
            dma((2, 2, nr + 1)),
            dma((2, 2, nr + 1)),
            dma((nz, nx)),
            dma((nz, nx)),
            dma((nz,)),
            dma((nz,)),
            dma((nz,)),
            dma((nz,)),
            dma((2, nseq)),
            dma((2, nseq)),
            dma((2, nx)),
            dma((2, nx)),
            dma((2, ny)),
            dma((2, ny)),
            dma((ny,)),
            dma((ny,)),
            dma((ny,)),
            dma((ny,)),
        ],
        compiler_params=pltpu.CompilerParams(
            collective_id=0, has_side_effects=True, vmem_limit_bytes=50 * 2**20
        ),
        cost_estimate=pl.CostEstimate(
            flops=4 * rows * feat * cols * ny, bytes_accessed=8 * rows * feat, transcendentals=0
        ),
    )(
        text_embed,
        image_rows,
        token_source.reshape(1, tok),
        slot_dest.reshape(1, slots),
        norm_gain.reshape(1, feat),
        kv_weight,
        kv_cot,
    )


def solution(mesh):
    both = P(("sec", "seq"), "tp")
    rows = P(("sec", "seq"))
    return jax.shard_map(
        per_device,
        mesh=mesh,
        in_specs=(both, both, rows, rows, P("tp"), both, both),
        out_specs=(both, both, both),
        check_vma=False,
    )
```

```python
import functools

import jax
import jax.numpy as jnp
from jax import lax
from jax.experimental import pallas as pl
from jax.experimental.pallas import tpu as pltpu
from jax.sharding import PartitionSpec as P

D = 8192
EPS = 1e-06
F32 = jnp.float32
BF16 = jnp.bfloat16
MESH = pl.DeviceIdType.MESH
LANES = 128


class Pair:
    def __init__(self, out, into):
        self.ends = (out, into)

    def __getitem__(self, i):
        return self.ends[i]()


def shift_of(n):
    return n.bit_length() - 1


def places(row, log_owner, nx, nseq):
    n = row.shape[1]
    own = lax.shift_right_arithmetic(row, jnp.full_like(row, log_owner))
    own_row = own.astype(F32)
    ii = lax.broadcasted_iota(jnp.int32, (n, n), 0)
    jj = lax.broadcasted_iota(jnp.int32, (n, n), 1)
    own_col = jnp.sum(jnp.where(ii == jj, own_row, 0.0), axis=1, keepdims=True)
    eq = own_col == own_row
    rank_row = jnp.sum(jnp.where(eq & (ii < jj), 1.0, 0.0), axis=0, keepdims=True)
    rank_col = jnp.sum(jnp.where(eq & (jj < ii), 1.0, 0.0), axis=1, keepdims=True)
    x_of = lax.shift_right_arithmetic(own, jnp.full_like(own, shift_of(nseq)))
    s_of = own & (nseq - 1)
    key = ((s_of * nx + x_of) * 2).astype(F32) + rank_row
    key = jnp.where(own_row >= 0.0, key, -1.0)
    pos = jnp.where(own_col >= 0.0, own_col * 2.0 + rank_col, -1.0)
    return key, pos, own_col


NEAR = (0, 3, -3, 6, -6)
ORDER = [(0, None)] + [(n, None) for n in NEAR[1:]] + [(n + e, (e, i)) for i, n in enumerate(NEAR) for e in (1, -1)] + [(8, None)]
LAG1, LAG2 = 3, 6
SLOT = {(n + 16) % 16: j for j, (n, _) in enumerate(ORDER)}


def kernel(
    nx, nz, ny,
    text_h, img_h, ts_h, sd_h, gain_h, w_h, cot_h,
    kv_out, tg_out, ig_out,
    text, img, ts, sd, gain, w, cot,
    wq, xg, cots, sq, acc, kvp, rs_send, rs_recv, sum_send, sum_recv,
    b1a, r1a, b2a, r2a, b1b, r1b, b2b, r2b,
    in_sem, z1_s, z1_r, z2_s, z2_r, z8_s, z8_r, x_s, x_r, sib_s, sib_r,
    e1_s, e1_r, e2_s, e2_r, yc_s, yc_r, rs_s, rs_r, sm_s, sm_r,
):
    x, s, y = lax.axis_index("sec"), lax.axis_index("seq"), lax.axis_index("tp")
    z, c = s // 2, s % 2
    nseq = 2 * nz
    tok, feat = text.shape
    slots = img.shape[0]
    rows = tok + slots
    cols = cot.shape[1]
    halves = cols // LANES
    npos = 2 * nx * nseq
    half = feat // 2

    def remote(src, dst, ss, rs, dev):
        return pltpu.make_async_remote_copy(
            src_ref=src, dst_ref=dst, send_sem=ss, recv_sem=rs, device_id=dev, device_id_type=MESH
        )

    def loop(lo, hi, body):
        if hi > lo:
            lax.fori_loop(lo, hi, lambda i, t: (body(i), t)[1], 0)

    pairs = [(w_h, w), (ts_h, ts), (cot_h, cot), (sd_h, sd), (gain_h, gain), (text_h, text), (img_h, img)]
    fetch = [pltpu.make_async_copy(p, q, in_sem.at[i]) for i, (p, q) in enumerate(pairs)]
    for f in fetch:
        f.start()

    barrier = pltpu.get_barrier_semaphore()

    def greet(dev):
        pl.semaphore_signal(barrier, inc=1, device_id=dev, device_id_type=MESH)

    loop(1, nseq, lambda k: greet((x, lax.rem(s + k, nseq), y)))
    for k in range(1, nx):
        greet((lax.rem(x + k, nx), s, y))
    for k in range(1, ny):
        greet((x, s, lax.rem(y + k, ny)))

    def at_z(o):
        return lax.rem(z + (o + nz) % nz, nz)

    def at_x(o):
        return lax.rem(x + (o + nx) % nx, nx)

    sib = (x, s + 1 - 2 * c, y)

    def copy_z1(i):
        n = NEAR[i]
        own, got = wq.at[x, 0, c], wq.at[x, i, c]
        dev = (x, 2 * at_z(-n) + c, y)
        return Pair(
            lambda: remote(own, got, z1_s.at[i], z1_r.at[i], dev),
            lambda: remote(got, got, z1_s.at[i], z1_r.at[i], dev),
        )

    def copy_z2(e, i):
        n, m = NEAR[i], (1 - e) // 2
        out, got = wq.at[x, i, c], wq.at[x, SLOT[(n + e) % 16], c]
        dev = (x, 2 * at_z(-e) + c, y)
        return Pair(
            lambda: remote(out, got, z2_s.at[m, i], z2_r.at[m, i], dev),
            lambda: remote(got, got, z2_s.at[m, i], z2_r.at[m, i], dev),
        )

    def copy_z8(m):
        n, to = (3, -2) if m == 0 else (4, 2)
        part = pl.ds(m * (half // 2), half // 2)
        out, got = wq.at[x, n, c, :, part], wq.at[x, SLOT[8], c, :, part]
        dev = (x, 2 * at_z(to) + c, y)
        return Pair(
            lambda: remote(out, got, z8_s.at[m], z8_r.at[m], dev),
            lambda: remote(got, got, z8_s.at[m], z8_r.at[m], dev),
        )

    def copy_x(j, m):
        up = m == 0 or (m == 2 and j % 2 == 0)
        frm = 0 if m < 2 else (-1 if up else 1)
        out = wq.at[at_x(frm), j, c]
        got = wq.at[at_x(frm + (-1 if up else 1)), j, c]
        dev = (at_x(1 if up else -1), s, y)
        return Pair(
            lambda: remote(out, out, x_s.at[j, m], x_r.at[j, m], dev),
            lambda: remote(got, got, x_s.at[j, m], x_r.at[j, m], dev),
        )

    def copy_sib(j):
        out, got = wq.at[:, j, c], wq.at[:, j, 1 - c]
        return Pair(
            lambda: remote(out, out, sib_s.at[j], sib_r.at[j], sib),
            lambda: remote(got, got, sib_s.at[j], sib_r.at[j], sib),
        )

    fetch[0].wait()
    w8 = w[...].astype(F32)
    wq[x, 0, c] = jnp.concatenate([w8[:, :half], w8[:, half:]], axis=0).astype(BF16)
    pl.semaphore_wait(barrier, nseq - 1 + nx - 1 + ny - 1)
    for i in range(1, 5):
        copy_z1(i)[0].start()
    copy_x(0, 0)[0].start()
    copy_x(0, 1)[0].start()
    copy_z2(1, 0)[0].start()
    copy_z2(-1, 0)[0].start()

    def pick_rows(key):
        n = key.shape[1]
        return jnp.where(lax.broadcasted_iota(jnp.int32, (npos, n), 0).astype(F32) == key, 1.0, 0.0).astype(BF16)

    def pick_cols(pos):
        n = pos.shape[0]
        return jnp.where(lax.broadcasted_iota(jnp.int32, (n, npos), 1).astype(F32) == pos, 1.0, 0.0).astype(BF16)

    def fill1(key, values, b1, r1):
        g = jnp.dot(pick_rows(key), values, preferred_element_type=F32)
        parts = [g[:, h * LANES : (h + 1) * LANES].reshape(nseq, 2 * nx, LANES) for h in range(halves)]
        b1[...] = jnp.concatenate(parts, axis=1).astype(BF16)
        r1[s] = b1[s]

    def fill2(r1, b2, r2):
        r = r1[...].astype(F32)
        m = jnp.concatenate(
            [r[:, h * 2 * nx : (h + 1) * 2 * nx].reshape(npos, LANES) for h in range(halves)], axis=1
        ).astype(BF16)
        i = lax.broadcasted_iota(jnp.int32, (npos, npos), 0)
        j = lax.broadcasted_iota(jnp.int32, (npos, npos), 1)
        lx, ls = shift_of(2 * nseq), shift_of(nseq)
        i_x = lax.shift_right_arithmetic(i, jnp.full_like(i, lx))
        i_s = lax.shift_right_arithmetic(i, jnp.full_like(i, 1)) & (nseq - 1)
        perm = jnp.where((i_s * nx + i_x) * 2 + (i & 1) == j, 1.0, 0.0).astype(BF16)
        b2[...] = jnp.dot(perm, m, preferred_element_type=F32).astype(BF16).reshape(nx, 2 * nseq, cols)
        r2[x] = b2[x]

    def take(pos, r2):
        return jnp.dot(pick_cols(pos), r2[...].reshape(npos, cols), preferred_element_type=F32)

    def copy1(n, b1, r1, k):
        to, frm = lax.rem(s + k, nseq), lax.rem(s + nseq - k, nseq)
        return Pair(
            lambda: remote(b1.at[to], r1.at[s], e1_s.at[n, k], e1_r.at[n, k], (x, to, y)),
            lambda: remote(b1.at[to], r1.at[frm], e1_s.at[n, k], e1_r.at[n, k], (x, to, y)),
        )

    def copy2(n, b2, r2, k):
        to, frm = lax.rem(x + k, nx), lax.rem(x + nx - k, nx)
        return Pair(
            lambda: remote(b2.at[to], r2.at[x], e2_s.at[n, k], e2_r.at[n, k], (to, s, y)),
            lambda: remote(b2.at[to], r2.at[frm], e2_s.at[n, k], e2_r.at[n, k], (to, s, y)),
        )

    def copy_y(part, k):
        to, frm = lax.rem(y + k, ny), lax.rem(y + ny - k, ny)
        at = pl.ds(0, tok) if part == 0 else pl.ds(tok, slots)
        return Pair(
            lambda: remote(cots.at[y, at], cots.at[y, at], yc_s.at[part, k], yc_r.at[part, k], (x, s, to)),
            lambda: remote(cots.at[y, at], cots.at[frm, at], yc_s.at[part, k], yc_r.at[part, k], (x, s, to)),
        )

    def copy_rs(grp, part, k):
        at = pl.ds(0, tok) if part == 0 else pl.ds(tok, slots)
        to = lax.rem(y + k, ny)
        return remote(
            rs_send.at[grp, k, at], rs_recv.at[grp, k, at], rs_s.at[grp, part, k], rs_r.at[grp, part, k], (x, s, to)
        )

    def copy_sum(n, k):
        to = lax.rem(y + k, ny)
        return remote(sum_send.at[n], sum_recv.at[n, k], sm_s.at[n, k], sm_r.at[n, k], (x, s, to))

    p = lax.broadcasted_iota(jnp.int32, (1, cols), 1)
    up_by = jnp.zeros_like(p)
    for j, (n, _) in enumerate(ORDER):
        up_by = jnp.where(lax.shift_right_arithmetic(p, jnp.full_like(p, 4)) == j, n + nz, up_by)
    place_of = ((z + up_by) & (nz - 1)) * 16 + (p & 15)
    reorder = jnp.where(lax.broadcasted_iota(jnp.int32, (cols, cols), 0) == place_of, 1.0, 0.0).astype(BF16)

    def to_pieces(v):
        return jnp.dot(v, reorder, preferred_element_type=F32).astype(BF16)

    def to_columns(v):
        return lax.dot_general(v, reorder, (((1,), (1,)), ((), ())), preferred_element_type=F32).astype(BF16)

    fetch[1].wait()
    fetch[2].wait()
    key_tok, pos_tok, own_tok = places(ts[...], shift_of(slots), nx, nseq)
    fill1(key_tok, cot[...], b1a, r1a)
    cots[y, :tok] = to_pieces(cot[...])

    def prepare(ref, base, lo, hi):
        def body(i):
            r = ref[pl.ds(pl.multiple_of(i * 16, 16), 16), :].astype(F32)
            at = pl.ds(pl.multiple_of(base + i * 16, 16), 16)
            xg[at, :] = (r * gain[...]).astype(BF16)
            sq[at, :] = jnp.broadcast_to(jnp.sum(r * r, axis=1, keepdims=True), (16, LANES))

        loop(lo, hi, body)

    work = {}
    for n in range(4):
        b = tok // 64
        work[2 + n] = [functools.partial(prepare, text, 0, n * b, (n + 1) * b)]
    for n in range(2):
        b = slots // 32
        work[6 + n] = [functools.partial(prepare, img, tok, n * b, (n + 1) * b)]

    def send_squares():
        sum_send[0] = jnp.transpose(sq[...])[:8]
        for k in range(1, ny):
            copy_sum(0, k).start()

    work[8] = [send_squares]

    def middle():
        loop(1, nseq, lambda k: copy1(0, b1a, r1a, k)[1].wait_recv())
        fill2(r1a, b2a, r2a)
        for k in range(1, nx):
            copy2(0, b2a, r2a, k)[0].start()

    work[9] = [middle]
    keys = []

    def slot_cots():
        keys.append(places(sd[...], shift_of(tok), nx, nseq))
        for k in range(1, nx):
            copy2(0, b2a, r2a, k)[1].wait_recv()
        cots[y, tok:] = to_pieces(take(keys[0][1], r2a).astype(BF16))
        for k in range(1, ny):
            copy_y(1, k)[0].start()

    work[13] = [slot_cots]

    def weights(t, grp, h):
        lo, hi = (0, nz) if grp is None else (grp * (nz // 2), (grp + 1) * (nz // 2))
        return wq[t, lo:hi, :, 8 * h : 8 * h + 8, :].reshape(16 * (hi - lo), half)

    dots = {0: jnp.zeros((tok, 1), F32), 1: jnp.zeros((slots, 1), F32)}

    def forward(grp):
        for j in range(grp * (nz // 2), (grp + 1) * (nz // 2)):
            copy_sib(j)[1].wait_recv()
        lanes = slice(grp * LANES, (grp + 1) * LANES)
        for part in (1, 0):
            lo, hi = (0, tok) if part == 0 else (tok, rows)
            v = jnp.zeros((hi - lo, ny * LANES), F32)
            for h in range(2):
                rhs = jnp.concatenate([weights(lax.rem(y + k, ny), grp, h) for k in range(ny)], axis=0)
                v = v + lax.dot_general(
                    xg[lo:hi, h * half : (h + 1) * half], rhs, (((1,), (1,)), ((), ())), preferred_element_type=F32
                )
            for k in (2, 1, 3, 0):
                u = v[:, k * LANES : (k + 1) * LANES]
                if k:
                    rs_send[grp, k, lo:hi] = u.astype(BF16)
                    copy_rs(grp, part, k).start()
                else:
                    kvp[lo:hi, lanes] = u
                near = cots[lax.rem(y + k, ny), lo:hi, lanes].astype(F32)
                dots[part] = dots[part] + jnp.sum(u * near, axis=1, keepdims=True)

    def forward_first():
        for part in range(2):
            for k in range(1, ny):
                copy_y(part, k)[1].wait_recv()
        forward(0)

    pieces = len(ORDER)
    work[pieces + LAG1 - 1] = [forward_first]
    for j in range(pieces + LAG2):
        if 1 <= j < 5:
            copy_z1(j)[1].wait_recv()
            copy_z2(1, j)[0].start()
            copy_z2(-1, j)[0].start()
            if j >= 3:
                copy_z8(j - 3)[0].start()
        elif 5 <= j < pieces - 1:
            copy_z2(*ORDER[j][1])[1].wait_recv()
        elif j == pieces - 1:
            copy_z8(0)[1].wait_recv()
            copy_z8(1)[1].wait_recv()
        if 1 <= j < pieces:
            copy_x(j, 0)[0].start()
            copy_x(j, 1)[0].start()
        if j == 4:
            loop(1, nseq, lambda k: copy1(0, b1a, r1a, k)[0].start())
            for k in range(1, ny):
                copy_y(0, k)[0].start()
        if LAG1 <= j < pieces + LAG1:
            i = j - LAG1
            copy_x(i, 0)[1].wait_recv()
            copy_x(i, 1)[1].wait_recv()
            copy_x(i, 2)[0].start()
        if LAG2 <= j:
            copy_x(j - LAG2, 2)[1].wait_recv()
            copy_sib(j - LAG2)[0].start()
        if j == 1:
            for f in fetch[3:]:
                f.wait()
        for f in work.get(j, ()):
            f()
    key_slot, pos_slot, own_slot = keys[0]

    total = sum_send[0]
    for k in range(1, ny):
        copy_sum(0, k).wait_recv()
        total = total + sum_recv[0, k]
    scale_r = lax.rsqrt(total[0:1] / D + EPS)
    sq[...] = jnp.transpose(jnp.broadcast_to(scale_r, (LANES, rows)))
    forward(1)

    def reduced(part):
        lo, hi = (0, tok) if part == 0 else (tok, rows)
        raw = kvp[lo:hi]
        for k in range(1, ny):
            for grp in range(2):
                copy_rs(grp, part, k).wait_recv()
            raw = raw + jnp.concatenate([rs_recv[0, k, lo:hi], rs_recv[1, k, lo:hi]], axis=1).astype(F32)
        return to_columns((raw * sq[lo:hi, 0:1]).astype(BF16))

    sum_send[1] = jnp.transpose(jnp.broadcast_to(jnp.concatenate([dots[0], dots[1]], axis=0), (rows, LANES)))[:8]
    for k in range(1, ny):
        copy_sum(1, k).start()

    fill1(key_slot, reduced(1), b1b, r1b)
    loop(1, nseq, lambda k: copy1(1, b1b, r1b, k)[0].start())

    cot_all = jnp.concatenate([cots[t] for t in range(ny)], axis=1)
    for h in range(2):
        rhs = jnp.concatenate([weights(t, None, h) for t in range(ny)], axis=0)
        acc[:, h * half : (h + 1) * half] = jnp.dot(cot_all, rhs, preferred_element_type=F32)

    total = sum_send[1]
    for k in range(1, ny):
        copy_sum(1, k).wait_recv()
        total = total + sum_recv[1, k]
    coef_r = scale_r * scale_r * scale_r * total[0:1] / D
    coef = jnp.transpose(jnp.broadcast_to(coef_r, (LANES, rows)))
    keep = jnp.concatenate([jnp.where(own_tok < 0.0, 1.0, 0.0), jnp.where(own_slot >= 0.0, 1.0, 0.0)], axis=0)
    lane = lax.broadcasted_iota(jnp.int32, (rows, LANES), 1)
    sq[...] = jnp.where(lane == 0, sq[...], jnp.where(lane == 1, coef, keep))

    def grads(ref, base, out):
        def body(i):
            here = pl.ds(pl.multiple_of(i * 16, 16), 16)
            at = pl.ds(pl.multiple_of(base + i * 16, 16), 16)
            r = ref[here, :].astype(F32)
            f = sq[at, :]
            g = f[:, 0:1] * (gain[...] * acc[at, :]) - r * f[:, 1:2]
            out[here, :] = jnp.where(f[:, 2:3] > 0.0, g, 0.0).astype(BF16)

        loop(0, ref.shape[0] // 16, body)

    loop(1, nseq, lambda k: copy1(1, b1b, r1b, k)[1].wait_recv())
    fill2(r1b, b2b, r2b)
    for k in range(1, nx):
        copy2(1, b2b, r2b, k)[0].start()
    grads(text, 0, tg_out)
    grads(img, tok, ig_out)
    kv_text = reduced(0)
    for i in range(1, 5):
        copy_z1(i)[0].wait_send()
    for i in range(5):
        copy_z2(1, i)[0].wait_send()
        copy_z2(-1, i)[0].wait_send()
    for m in range(2):
        copy_z8(m)[0].wait_send()
    for j in range(pieces):
        for m in range(3):
            copy_x(j, m)[0].wait_send()
        copy_sib(j)[0].wait_send()
    for k in range(1, nx):
        copy2(0, b2a, r2a, k)[0].wait_send()
    for k in range(1, ny):
        for part in range(2):
            copy_y(part, k)[0].wait_send()
            copy_rs(0, part, k).wait_send()
            copy_rs(1, part, k).wait_send()
            copy_sum(part, k).wait_send()

    def sent1(k):
        copy1(0, b1a, r1a, k)[0].wait_send()
        copy1(1, b1b, r1b, k)[0].wait_send()

    loop(1, nseq, sent1)

    for k in range(1, nx):
        copy2(1, b2b, r2b, k)[1].wait_recv()
    got = take(pos_tok, r2b)
    kv_out[...] = jnp.where(own_tok >= 0.0, got, kv_text.astype(F32)).astype(BF16)
    for k in range(1, nx):
        copy2(1, b2b, r2b, k)[0].wait_send()


def flush(a, b, c, out_a, out_b, out_c, via_a, via_b, via_c, sem):
    ways = ((b, via_b, out_b), (c, via_c, out_c), (a, via_a, out_a))
    into = [pltpu.make_async_copy(p, v, sem.at[0, i]) for i, (p, v, _) in enumerate(ways)]
    away = [pltpu.make_async_copy(v, q, sem.at[1, i]) for i, (_, v, q) in enumerate(ways)]
    for p in into:
        p.start()
    for p, q in zip(into, away):
        p.wait()
        q.start()
    for q in away:
        q.wait()


def per_device(text_embed, image_rows, token_source, slot_dest, norm_gain, kv_weight, kv_cot):
    nx, nseq, ny = lax.axis_size("sec"), lax.axis_size("seq"), lax.axis_size("tp")
    nz = nseq // 2
    tok, feat = text_embed.shape
    slots = image_rows.shape[0]
    rows = tok + slots
    cols = kv_cot.shape[1]
    dma = pltpu.SemaphoreType.DMA
    blk = (2 * nx * cols) // LANES
    exch = [
        pltpu.VMEM((nseq, blk, LANES), BF16),
        pltpu.VMEM((nseq, blk, LANES), BF16),
        pltpu.VMEM((nx, 2 * nseq, cols), BF16),
        pltpu.VMEM((nx, 2 * nseq, cols), BF16),
    ]
    vmem = pl.BlockSpec(memory_space=pltpu.VMEM)
    outs = pl.pallas_call(
        functools.partial(kernel, nx, nz, ny),
        out_shape=(
            jax.ShapeDtypeStruct((tok, cols), BF16),
            jax.ShapeDtypeStruct((tok, feat), BF16),
            jax.ShapeDtypeStruct((slots, feat), BF16),
        ),
        in_specs=[pl.BlockSpec(memory_space=pl.ANY)] * 7,
        out_specs=(vmem, vmem, vmem),
        scratch_shapes=[
            pltpu.VMEM((tok, feat), BF16),
            pltpu.VMEM((slots, feat), BF16),
            pltpu.VMEM((1, tok), jnp.int32),
            pltpu.VMEM((1, slots), jnp.int32),
            pltpu.VMEM((1, feat), F32),
            pltpu.VMEM((8, feat), BF16),
            pltpu.VMEM((tok, cols), BF16),
            pltpu.VMEM((nx, nz, 2, 16, feat // 2), BF16),
            pltpu.VMEM((rows, feat), BF16),
            pltpu.VMEM((ny, rows, cols), BF16),
            pltpu.VMEM((rows, LANES), F32),
            pltpu.VMEM((rows, feat), F32),
            pltpu.VMEM((rows, cols), F32),
            pltpu.VMEM((2, ny, rows, LANES), BF16),
            pltpu.VMEM((2, ny, rows, LANES), BF16),
            pltpu.VMEM((2, 8, rows), F32),
            pltpu.VMEM((2, ny, 8, rows), F32),
            *exch,
            *exch,
            dma((7,)),
            *[dma((5,))] * 2,
            *[dma((2, 5))] * 2,
            *[dma((2,))] * 2,
            *[dma((nz, 3))] * 2,
            *[dma((nz,))] * 2,
            *[dma((2, nseq))] * 2,
            *[dma((2, nx))] * 2,
            *[dma((2, ny))] * 2,
            *[dma((2, 2, ny))] * 2,
            *[dma((2, ny))] * 2,
        ],
        compiler_params=pltpu.CompilerParams(
            collective_id=0, has_side_effects=True, vmem_limit_bytes=58 * 2**20
        ),
        cost_estimate=pl.CostEstimate(
            flops=4 * rows * feat * cols * ny, bytes_accessed=8 * rows * feat, transcendentals=0
        ),
    )(
        text_embed,
        image_rows,
        token_source.reshape(1, tok),
        slot_dest.reshape(1, slots),
        norm_gain.reshape(1, feat),
        kv_weight,
        kv_cot,
    )
    where = pl.BlockSpec(memory_space=pl.ANY)
    return pl.pallas_call(
        flush,
        out_shape=tuple(jax.ShapeDtypeStruct(o.shape, o.dtype) for o in outs),
        in_specs=[where] * 3,
        out_specs=(where,) * 3,
        scratch_shapes=[*[pltpu.VMEM(o.shape, o.dtype) for o in outs], dma((2, 3))],
        compiler_params=pltpu.CompilerParams(vmem_limit_bytes=58 * 2**20),
    )(*outs)


def solution(mesh):
    both = P(("sec", "seq"), "tp")
    rows = P(("sec", "seq"))
    return jax.shard_map(
        per_device,
        mesh=mesh,
        in_specs=(both, both, rows, rows, P("tp"), both, both),
        out_specs=(both, both, both),
        check_vma=False,
    )
```

```python
import functools

import jax
import jax.numpy as jnp
from jax import lax
from jax.experimental import pallas as pl
from jax.experimental.pallas import tpu as pltpu
from jax.sharding import PartitionSpec as P

D = 8192
EPS = 1e-06
F32 = jnp.float32
BF16 = jnp.bfloat16
MESH = pl.DeviceIdType.MESH
LANES = 128


class Pair:
    def __init__(self, out, into):
        self.ends = (out, into)

    def __getitem__(self, i):
        return self.ends[i]()


def shift_of(n):
    return n.bit_length() - 1


def places(row, log_owner, nx, nseq):
    n = row.shape[1]
    own = lax.shift_right_arithmetic(row, jnp.full_like(row, log_owner))
    own_row = own.astype(F32)
    ii = lax.broadcasted_iota(jnp.int32, (n, n), 0)
    jj = lax.broadcasted_iota(jnp.int32, (n, n), 1)
    own_col = jnp.sum(jnp.where(ii == jj, own_row, 0.0), axis=1, keepdims=True)
    eq = own_col == own_row
    rank_row = jnp.sum(jnp.where(eq & (ii < jj), 1.0, 0.0), axis=0, keepdims=True)
    rank_col = jnp.sum(jnp.where(eq & (jj < ii), 1.0, 0.0), axis=1, keepdims=True)
    x_of = lax.shift_right_arithmetic(own, jnp.full_like(own, shift_of(nseq)))
    s_of = own & (nseq - 1)
    key = ((s_of * nx + x_of) * 2).astype(F32) + rank_row
    key = jnp.where(own_row >= 0.0, key, -1.0)
    pos = jnp.where(own_col >= 0.0, own_col * 2.0 + rank_col, -1.0)
    return key, pos, own_col


NEAR = (0, 3, -3, 6, -6)
ORDER = (
    [(0, (0, 0)), (1, (1, 0)), (-1, (-1, 0))]
    + [(NEAR[i], (0, i)) for i in range(1, 5)]
    + [(NEAR[i] + e, (e, i)) for i in range(1, 5) for e in (1, -1)]
    + [(8, None)]
)
LAG1, LAG2, EXCH = 3, 6, 12
SLOT = {(n + 16) % 16: j for j, (n, _) in enumerate(ORDER)}


def kernel(
    nx, nz, ny,
    text_h, img_h, ts_h, sd_h, gain_h, w_h, cot_h,
    kv_out, tg_out, ig_out,
    text, img, ts, sd, gain, w, cot,
    wq, xg, cots, sq, acc, vs, kvp, rs_send, rs_recv, sum_send, sum_recv,
    b1a, r1a, b2a, r2a, b1b, r1b, b2b, r2b,
    in_sem, z1_s, z1_r, z2_s, z2_r, z8_s, z8_r, x_s, x_r, sib_s, sib_r,
    e1_s, e1_r, e2_s, e2_r, yc_s, yc_r, rs_s, rs_r, sm_s, sm_r,
):
    x, s, y = lax.axis_index("sec"), lax.axis_index("seq"), lax.axis_index("tp")
    z, c = s // 2, s % 2
    nseq = 2 * nz
    tok, feat = text.shape
    slots = img.shape[0]
    rows = tok + slots
    cols = cot.shape[1]
    halves = cols // LANES
    npos = 2 * nx * nseq
    half = feat // 2

    def remote(src, dst, ss, rs, dev):
        return pltpu.make_async_remote_copy(
            src_ref=src, dst_ref=dst, send_sem=ss, recv_sem=rs, device_id=dev, device_id_type=MESH
        )

    def loop(lo, hi, body):
        if hi > lo:
            lax.fori_loop(lo, hi, lambda i, t: (body(i), t)[1], 0)

    pairs = [(w_h, w), (ts_h, ts), (cot_h, cot), (sd_h, sd), (gain_h, gain), (text_h, text), (img_h, img)]
    fetch = [pltpu.make_async_copy(p, q, in_sem.at[i]) for i, (p, q) in enumerate(pairs)]
    for f in fetch:
        f.start()

    barrier = pltpu.get_barrier_semaphore()

    def greet(dev):
        pl.semaphore_signal(barrier, inc=1, device_id=dev, device_id_type=MESH)

    loop(1, nseq, lambda k: greet((x, lax.rem(s + k, nseq), y)))
    for k in range(1, nx):
        greet((lax.rem(x + k, nx), s, y))
    for k in range(1, ny):
        greet((x, s, lax.rem(y + k, ny)))

    def at_z(o):
        return lax.rem(z + (o + nz) % nz, nz)

    def at_x(o):
        return lax.rem(x + (o + nx) % nx, nx)

    sib = (x, s + 1 - 2 * c, y)

    def copy_z1(i):
        n = NEAR[i]
        own, got = wq.at[x, 0, c], wq.at[x, SLOT[n % 16], c]
        dev = (x, 2 * at_z(-n) + c, y)
        return Pair(
            lambda: remote(own, got, z1_s.at[i], z1_r.at[i], dev),
            lambda: remote(got, got, z1_s.at[i], z1_r.at[i], dev),
        )

    def copy_z2(e, i):
        n, m = NEAR[i], (1 - e) // 2
        out, got = wq.at[x, SLOT[n % 16], c], wq.at[x, SLOT[(n + e) % 16], c]
        dev = (x, 2 * at_z(-e) + c, y)
        return Pair(
            lambda: remote(out, got, z2_s.at[m, i], z2_r.at[m, i], dev),
            lambda: remote(got, got, z2_s.at[m, i], z2_r.at[m, i], dev),
        )

    def copy_z8(m):
        n, to = (6, -2) if m == 0 else (-6, 2)
        part = pl.ds(m * (half // 2), half // 2)
        out, got = wq.at[x, SLOT[n % 16], c, :, part], wq.at[x, SLOT[8], c, :, part]
        dev = (x, 2 * at_z(to) + c, y)
        return Pair(
            lambda: remote(out, got, z8_s.at[m], z8_r.at[m], dev),
            lambda: remote(got, got, z8_s.at[m], z8_r.at[m], dev),
        )

    def copy_x(j, m):
        up = m == 0 or (m == 2 and j % 2 == 0)
        frm = 0 if m < 2 else (-1 if up else 1)
        out = wq.at[at_x(frm), j, c]
        got = wq.at[at_x(frm + (-1 if up else 1)), j, c]
        dev = (at_x(1 if up else -1), s, y)
        return Pair(
            lambda: remote(out, out, x_s.at[j, m], x_r.at[j, m], dev),
            lambda: remote(got, got, x_s.at[j, m], x_r.at[j, m], dev),
        )

    def copy_sib(j):
        out, got = wq.at[:, j, c], wq.at[:, j, 1 - c]
        return Pair(
            lambda: remote(out, out, sib_s.at[j], sib_r.at[j], sib),
            lambda: remote(got, got, sib_s.at[j], sib_r.at[j], sib),
        )

    fetch[0].wait()
    w8 = w[...].astype(F32)
    wq[x, 0, c] = jnp.concatenate([w8[:, :half], w8[:, half:]], axis=0).astype(BF16)
    pl.semaphore_wait(barrier, nseq - 1 + nx - 1 + ny - 1)
    copy_z2(1, 0)[0].start()
    copy_z2(-1, 0)[0].start()
    copy_x(0, 0)[0].start()
    copy_x(0, 1)[0].start()
    for i in range(1, 5):
        copy_z1(i)[0].start()

    def pick_rows(key):
        n = key.shape[1]
        return jnp.where(lax.broadcasted_iota(jnp.int32, (npos, n), 0).astype(F32) == key, 1.0, 0.0).astype(BF16)

    def pick_cols(pos):
        n = pos.shape[0]
        return jnp.where(lax.broadcasted_iota(jnp.int32, (n, npos), 1).astype(F32) == pos, 1.0, 0.0).astype(BF16)

    def fill1(key, values, b1, r1):
        g = jnp.dot(pick_rows(key), values, preferred_element_type=F32)
        parts = [g[:, h * LANES : (h + 1) * LANES].reshape(nseq, 2 * nx, LANES) for h in range(halves)]
        b1[...] = jnp.concatenate(parts, axis=1).astype(BF16)
        r1[s] = b1[s]

    def fill2(r1, b2, r2):
        r = r1[...].astype(F32)
        m = jnp.concatenate(
            [r[:, h * 2 * nx : (h + 1) * 2 * nx].reshape(npos, LANES) for h in range(halves)], axis=1
        ).astype(BF16)
        i = lax.broadcasted_iota(jnp.int32, (npos, npos), 0)
        j = lax.broadcasted_iota(jnp.int32, (npos, npos), 1)
        lx, ls = shift_of(2 * nseq), shift_of(nseq)
        i_x = lax.shift_right_arithmetic(i, jnp.full_like(i, lx))
        i_s = lax.shift_right_arithmetic(i, jnp.full_like(i, 1)) & (nseq - 1)
        perm = jnp.where((i_s * nx + i_x) * 2 + (i & 1) == j, 1.0, 0.0).astype(BF16)
        b2[...] = jnp.dot(perm, m, preferred_element_type=F32).astype(BF16).reshape(nx, 2 * nseq, cols)
        r2[x] = b2[x]

    def take(pos, r2):
        return jnp.dot(pick_cols(pos), r2[...].reshape(npos, cols), preferred_element_type=F32)

    def copy1(n, b1, r1, k):
        to, frm = lax.rem(s + k, nseq), lax.rem(s + nseq - k, nseq)
        return Pair(
            lambda: remote(b1.at[to], r1.at[s], e1_s.at[n, k], e1_r.at[n, k], (x, to, y)),
            lambda: remote(b1.at[to], r1.at[frm], e1_s.at[n, k], e1_r.at[n, k], (x, to, y)),
        )

    def copy2(n, b2, r2, k):
        to, frm = lax.rem(x + k, nx), lax.rem(x + nx - k, nx)
        return Pair(
            lambda: remote(b2.at[to], r2.at[x], e2_s.at[n, k], e2_r.at[n, k], (to, s, y)),
            lambda: remote(b2.at[to], r2.at[frm], e2_s.at[n, k], e2_r.at[n, k], (to, s, y)),
        )

    def copy_y(part, k):
        to, frm = lax.rem(y + k, ny), lax.rem(y + ny - k, ny)
        at = pl.ds(0, tok) if part == 0 else pl.ds(tok, slots)
        return Pair(
            lambda: remote(cots.at[y, at], cots.at[y, at], yc_s.at[part, k], yc_r.at[part, k], (x, s, to)),
            lambda: remote(cots.at[y, at], cots.at[frm, at], yc_s.at[part, k], yc_r.at[part, k], (x, s, to)),
        )

    def copy_rs(grp, part, k):
        at = pl.ds(0, tok) if part == 0 else pl.ds(tok, slots)
        to = lax.rem(y + k, ny)
        return remote(
            rs_send.at[grp, k, at], rs_recv.at[grp, k, at], rs_s.at[grp, part, k], rs_r.at[grp, part, k], (x, s, to)
        )

    def copy_sum(n, k):
        to = lax.rem(y + k, ny)
        return remote(sum_send.at[n], sum_recv.at[n, k], sm_s.at[n, k], sm_r.at[n, k], (x, s, to))

    p = lax.broadcasted_iota(jnp.int32, (1, cols), 1)
    up_by = jnp.zeros_like(p)
    for j, (n, _) in enumerate(ORDER):
        up_by = jnp.where(lax.shift_right_arithmetic(p, jnp.full_like(p, 4)) == j, n + nz, up_by)
    place_of = ((z + up_by) & (nz - 1)) * 16 + (p & 15)
    reorder = jnp.where(lax.broadcasted_iota(jnp.int32, (cols, cols), 0) == place_of, 1.0, 0.0).astype(BF16)

    def to_pieces(v):
        return jnp.dot(v, reorder, preferred_element_type=F32).astype(BF16)

    def to_columns(v):
        return lax.dot_general(v, reorder, (((1,), (1,)), ((), ())), preferred_element_type=F32).astype(BF16)

    fetch[1].wait()
    fetch[2].wait()
    key_tok, pos_tok, own_tok = places(ts[...], shift_of(slots), nx, nseq)
    fill1(key_tok, cot[...], b1a, r1a)
    cots[y, :tok] = to_pieces(cot[...])

    def prepare(ref, base, lo, hi):
        def body(i):
            r = ref[pl.ds(pl.multiple_of(i * 16, 16), 16), :].astype(F32)
            at = pl.ds(pl.multiple_of(base + i * 16, 16), 16)
            xg[at, :] = (r * gain[...]).astype(BF16)
            sq[at, :] = jnp.broadcast_to(jnp.sum(r * r, axis=1, keepdims=True), (16, LANES))

        loop(lo, hi, body)

    work = {}
    for n in range(4):
        b = tok // 64
        work[2 + n] = [functools.partial(prepare, text, 0, n * b, (n + 1) * b)]
    for n in range(2):
        b = slots // 32
        work[6 + n] = [functools.partial(prepare, img, tok, n * b, (n + 1) * b)]

    def send_squares():
        sum_send[0] = jnp.transpose(sq[...])[:8]
        for k in range(1, ny):
            copy_sum(0, k).start()

    work[8] = [send_squares]

    def middle():
        loop(1, nseq, lambda k: copy1(0, b1a, r1a, k)[1].wait_recv())
        fill2(r1a, b2a, r2a)
        for k in range(1, nx):
            copy2(0, b2a, r2a, k)[0].start()

    work[19] = [middle]
    keys = []

    def slot_cots():
        keys.append(places(sd[...], shift_of(tok), nx, nseq))
        for k in range(1, nx):
            copy2(0, b2a, r2a, k)[1].wait_recv()
        cots[y, tok:] = to_pieces(take(keys[0][1], r2a).astype(BF16))
        for k in range(1, ny):
            copy_y(1, k)[0].start()


    def weights(t, grp, h):
        lo, hi = (0, nz) if grp is None else (grp * (nz // 2), (grp + 1) * (nz // 2))
        return wq[t, lo:hi, :, 8 * h : 8 * h + 8, :].reshape(16 * (hi - lo), half)

    def forward(grp):
        for j in range(grp * (nz // 2), (grp + 1) * (nz // 2)):
            copy_sib(j)[1].wait_recv()
        lanes = slice(grp * LANES, (grp + 1) * LANES)
        for part in (1, 0):
            lo, hi = (0, tok) if part == 0 else (tok, rows)
            v = jnp.zeros((hi - lo, ny * LANES), F32)
            for h in range(2):
                rhs = jnp.concatenate([weights(lax.rem(y + k, ny), grp, h) for k in range(ny)], axis=0)
                v = v + lax.dot_general(
                    xg[lo:hi, h * half : (h + 1) * half], rhs, (((1,), (1,)), ((), ())), preferred_element_type=F32
                )
            for k in (2, 1, 3, 0):
                u = v[:, k * LANES : (k + 1) * LANES]
                if k:
                    rs_send[grp, k, lo:hi] = u.astype(BF16)
                    copy_rs(grp, part, k).start()
                else:
                    kvp[lo:hi, lanes] = u
                vs[grp, k, lo:hi] = u

    pieces = len(ORDER)
    work.setdefault(pieces + LAG1 - 1, []).append(functools.partial(forward, 0))
    for j in range(pieces + LAG2):
        if 1 <= j < pieces:
            come = ORDER[j][1]
            if come is None:
                copy_z8(0)[1].wait_recv()
                copy_z8(1)[1].wait_recv()
            elif come[0]:
                copy_z2(*come)[1].wait_recv()
            else:
                i = come[1]
                copy_z1(i)[1].wait_recv()
                copy_z2(1, i)[0].start()
                copy_z2(-1, i)[0].start()
                if i >= 3:
                    copy_z8(i - 3)[0].start()
            copy_x(j, 0)[0].start()
            copy_x(j, 1)[0].start()
        if j == 8:
            for k in range(1, ny):
                copy_y(0, k)[0].start()
        if j == EXCH:
            loop(1, nseq, lambda k: copy1(0, b1a, r1a, k)[0].start())
        if LAG1 <= j < pieces + LAG1:
            i = j - LAG1
            copy_x(i, 0)[1].wait_recv()
            copy_x(i, 1)[1].wait_recv()
            copy_x(i, 2)[0].start()
        if LAG2 <= j:
            copy_x(j - LAG2, 2)[1].wait_recv()
            copy_sib(j - LAG2)[0].start()
        if j == 1:
            for f in fetch[3:]:
                f.wait()
        for f in work.get(j, ()):
            f()

    total = sum_send[0]
    for k in range(1, ny):
        copy_sum(0, k).wait_recv()
        total = total + sum_recv[0, k]
    scale_r = lax.rsqrt(total[0:1] / D + EPS)
    sq[...] = jnp.transpose(jnp.broadcast_to(scale_r, (LANES, rows)))
    forward(1)
    slot_cots()
    key_slot, pos_slot, own_slot = keys[0]

    def reduced(part):
        lo, hi = (0, tok) if part == 0 else (tok, rows)
        raw = kvp[lo:hi]
        for k in range(1, ny):
            for grp in range(2):
                copy_rs(grp, part, k).wait_recv()
            raw = raw + jnp.concatenate([rs_recv[0, k, lo:hi], rs_recv[1, k, lo:hi]], axis=1).astype(F32)
        return to_columns((raw * sq[lo:hi, 0:1]).astype(BF16))

    fill1(key_slot, reduced(1), b1b, r1b)
    for k in range(1, nseq):
        copy1(1, b1b, r1b, k)[0].start()

    for part in range(2):
        for k in range(1, ny):
            copy_y(part, k)[1].wait_recv()
    dots = jnp.zeros((rows, LANES), F32)
    for k in range(ny):
        near = cots[lax.rem(y + k, ny)].astype(F32)
        for grp in range(2):
            dots = dots + vs[grp, k] * near[:, grp * LANES : (grp + 1) * LANES]
    sum_send[1] = jnp.transpose(jnp.broadcast_to(jnp.sum(dots, axis=1, keepdims=True), (rows, LANES)))[:8]
    for k in range(1, ny):
        copy_sum(1, k).start()

    cot_all = jnp.concatenate([cots[t] for t in range(ny)], axis=1)
    for h in range(2):
        rhs = jnp.concatenate([weights(t, None, h) for t in range(ny)], axis=0)
        acc[:, h * half : (h + 1) * half] = jnp.dot(cot_all, rhs, preferred_element_type=F32)

    total = sum_send[1]
    for k in range(1, ny):
        copy_sum(1, k).wait_recv()
        total = total + sum_recv[1, k]
    coef_r = scale_r * scale_r * scale_r * total[0:1] / D
    coef = jnp.transpose(jnp.broadcast_to(coef_r, (LANES, rows)))
    keep = jnp.concatenate([jnp.where(own_tok < 0.0, 1.0, 0.0), jnp.where(own_slot >= 0.0, 1.0, 0.0)], axis=0)
    lane = lax.broadcasted_iota(jnp.int32, (rows, LANES), 1)
    sq[...] = jnp.where(lane == 0, sq[...], jnp.where(lane == 1, coef, keep))

    def grads(ref, base, out):
        def body(i):
            here = pl.ds(pl.multiple_of(i * 16, 16), 16)
            at = pl.ds(pl.multiple_of(base + i * 16, 16), 16)
            r = ref[here, :].astype(F32)
            f = sq[at, :]
            g = f[:, 0:1] * (gain[...] * acc[at, :]) - r * f[:, 1:2]
            out[here, :] = jnp.where(f[:, 2:3] > 0.0, g, 0.0).astype(BF16)

        loop(0, ref.shape[0] // 16, body)

    loop(1, nseq, lambda k: copy1(1, b1b, r1b, k)[1].wait_recv())
    fill2(r1b, b2b, r2b)
    for k in range(1, nx):
        copy2(1, b2b, r2b, k)[0].start()
    grads(text, 0, tg_out)
    grads(img, tok, ig_out)
    kv_text = reduced(0)
    for i in range(1, 5):
        copy_z1(i)[0].wait_send()
    for i in range(5):
        copy_z2(1, i)[0].wait_send()
        copy_z2(-1, i)[0].wait_send()
    for m in range(2):
        copy_z8(m)[0].wait_send()
    for j in range(pieces):
        for m in range(3):
            copy_x(j, m)[0].wait_send()
        copy_sib(j)[0].wait_send()
    for k in range(1, nx):
        copy2(0, b2a, r2a, k)[0].wait_send()
    for k in range(1, ny):
        for part in range(2):
            copy_y(part, k)[0].wait_send()
            copy_rs(0, part, k).wait_send()
            copy_rs(1, part, k).wait_send()
            copy_sum(part, k).wait_send()

    def sent1(k):
        copy1(0, b1a, r1a, k)[0].wait_send()
        copy1(1, b1b, r1b, k)[0].wait_send()

    loop(1, nseq, sent1)

    for k in range(1, nx):
        copy2(1, b2b, r2b, k)[1].wait_recv()
    got = take(pos_tok, r2b)
    kv_out[...] = jnp.where(own_tok >= 0.0, got, kv_text.astype(F32)).astype(BF16)
    for k in range(1, nx):
        copy2(1, b2b, r2b, k)[0].wait_send()


def flush(a, b, c, out_a, out_b, out_c, via_a, via_b, via_c, sem):
    ways = ((b, via_b, out_b), (c, via_c, out_c), (a, via_a, out_a))
    into = [pltpu.make_async_copy(p, v, sem.at[0, i]) for i, (p, v, _) in enumerate(ways)]
    away = [pltpu.make_async_copy(v, q, sem.at[1, i]) for i, (_, v, q) in enumerate(ways)]
    for p in into:
        p.start()
    for p, q in zip(into, away):
        p.wait()
        q.start()
    for q in away:
        q.wait()


def per_device(text_embed, image_rows, token_source, slot_dest, norm_gain, kv_weight, kv_cot):
    nx, nseq, ny = lax.axis_size("sec"), lax.axis_size("seq"), lax.axis_size("tp")
    nz = nseq // 2
    tok, feat = text_embed.shape
    slots = image_rows.shape[0]
    rows = tok + slots
    cols = kv_cot.shape[1]
    dma = pltpu.SemaphoreType.DMA
    blk = (2 * nx * cols) // LANES
    exch = [
        pltpu.VMEM((nseq, blk, LANES), BF16),
        pltpu.VMEM((nseq, blk, LANES), BF16),
        pltpu.VMEM((nx, 2 * nseq, cols), BF16),
        pltpu.VMEM((nx, 2 * nseq, cols), BF16),
    ]
    vmem = pl.BlockSpec(memory_space=pltpu.VMEM)
    outs = pl.pallas_call(
        functools.partial(kernel, nx, nz, ny),
        out_shape=(
            jax.ShapeDtypeStruct((tok, cols), BF16),
            jax.ShapeDtypeStruct((tok, feat), BF16),
            jax.ShapeDtypeStruct((slots, feat), BF16),
        ),
        in_specs=[pl.BlockSpec(memory_space=pl.ANY)] * 7,
        out_specs=(vmem, vmem, vmem),
        scratch_shapes=[
            pltpu.VMEM((tok, feat), BF16),
            pltpu.VMEM((slots, feat), BF16),
            pltpu.VMEM((1, tok), jnp.int32),
            pltpu.VMEM((1, slots), jnp.int32),
            pltpu.VMEM((1, feat), F32),
            pltpu.VMEM((8, feat), BF16),
            pltpu.VMEM((tok, cols), BF16),
            pltpu.VMEM((nx, nz, 2, 16, feat // 2), BF16),
            pltpu.VMEM((rows, feat), BF16),
            pltpu.VMEM((ny, rows, cols), BF16),
            pltpu.VMEM((rows, LANES), F32),
            pltpu.VMEM((rows, feat), F32),
            pltpu.VMEM((2, ny, rows, LANES), F32),
            pltpu.VMEM((rows, cols), F32),
            pltpu.VMEM((2, ny, rows, LANES), BF16),
            pltpu.VMEM((2, ny, rows, LANES), BF16),
            pltpu.VMEM((2, 8, rows), F32),
            pltpu.VMEM((2, ny, 8, rows), F32),
            *exch,
            *exch,
            dma((7,)),
            *[dma((5,))] * 2,
            *[dma((2, 5))] * 2,
            *[dma((2,))] * 2,
            *[dma((nz, 3))] * 2,
            *[dma((nz,))] * 2,
            *[dma((2, nseq))] * 2,
            *[dma((2, nx))] * 2,
            *[dma((2, ny))] * 2,
            *[dma((2, 2, ny))] * 2,
            *[dma((2, ny))] * 2,
        ],
        compiler_params=pltpu.CompilerParams(
            collective_id=0, has_side_effects=True, vmem_limit_bytes=58 * 2**20
        ),
        cost_estimate=pl.CostEstimate(
            flops=4 * rows * feat * cols * ny, bytes_accessed=8 * rows * feat, transcendentals=0
        ),
    )(
        text_embed,
        image_rows,
        token_source.reshape(1, tok),
        slot_dest.reshape(1, slots),
        norm_gain.reshape(1, feat),
        kv_weight,
        kv_cot,
    )
    where = pl.BlockSpec(memory_space=pl.ANY)
    return pl.pallas_call(
        flush,
        out_shape=tuple(jax.ShapeDtypeStruct(o.shape, o.dtype) for o in outs),
        in_specs=[where] * 3,
        out_specs=(where,) * 3,
        scratch_shapes=[*[pltpu.VMEM(o.shape, o.dtype) for o in outs], dma((2, 3))],
        compiler_params=pltpu.CompilerParams(vmem_limit_bytes=58 * 2**20),
    )(*outs)


def solution(mesh):
    both = P(("sec", "seq"), "tp")
    rows = P(("sec", "seq"))
    return jax.shard_map(
        per_device,
        mesh=mesh,
        in_specs=(both, both, rows, rows, P("tp"), both, both),
        out_specs=(both, both, both),
        check_vma=False,
    )
```

```python
import functools

import jax
import jax.numpy as jnp
from jax import lax
from jax.experimental import pallas as pl
from jax.experimental.pallas import tpu as pltpu
from jax.sharding import PartitionSpec as P

D = 8192
EPS = 1e-06
F32 = jnp.float32
BF16 = jnp.bfloat16
MESH = pl.DeviceIdType.MESH
LANES = 128


class Pair:
    def __init__(self, out, into):
        self.ends = (out, into)

    def __getitem__(self, i):
        return self.ends[i]()


def shift_of(n):
    return n.bit_length() - 1


def places(row, log_owner, nx, nseq):
    n = row.shape[1]
    own = lax.shift_right_arithmetic(row, jnp.full_like(row, log_owner))
    own_row = own.astype(F32)
    ii = lax.broadcasted_iota(jnp.int32, (n, n), 0)
    jj = lax.broadcasted_iota(jnp.int32, (n, n), 1)
    own_col = jnp.sum(jnp.where(ii == jj, own_row, 0.0), axis=1, keepdims=True)
    eq = own_col == own_row
    rank_row = jnp.sum(jnp.where(eq & (ii < jj), 1.0, 0.0), axis=0, keepdims=True)
    rank_col = jnp.sum(jnp.where(eq & (jj < ii), 1.0, 0.0), axis=1, keepdims=True)
    x_of = lax.shift_right_arithmetic(own, jnp.full_like(own, shift_of(nseq)))
    s_of = own & (nseq - 1)
    key = ((s_of * nx + x_of) * 2).astype(F32) + rank_row
    key = jnp.where(own_row >= 0.0, key, -1.0)
    pos = jnp.where(own_col >= 0.0, own_col * 2.0 + rank_col, -1.0)
    return key, pos, own_col


NEAR = (0, 5, -5)
STEPS = (1, -1, 2, -2)
ORDER = (
    [(0, (0, 0))]
    + [(e, (e, 0)) for e in STEPS]
    + [(NEAR[i], (0, i)) for i in (1, 2)]
    + [(NEAR[i] + e, (e, i)) for e in STEPS for i in (1, 2)]
    + [(8, None)]
)
LAG1, LAG2, EXCH = 3, 6, 12
SLOT = {(n + 16) % 16: j for j, (n, _) in enumerate(ORDER)}


def kernel(
    nx, nz, ny,
    text_h, img_h, ts_h, sd_h, gain_h, w_h, cot_h,
    kv_h, tg_h, ig_h,
    kv_out, tg_out, ig_out,
    text, img, ts, sd, gain, w, cot,
    wq, xg, cots, sq, acc, vs, kvp, rs_send, rs_recv, sum_send, sum_recv,
    b1a, r1a, b2a, r2a, b1b, r1b, b2b, r2b,
    out_sem, in_sem, z1_s, z1_r, z2_s, z2_r, z8_s, z8_r, x_s, x_r, sib_s, sib_r,
    e1_s, e1_r, e2_s, e2_r, yc_s, yc_r, rs_s, rs_r, sm_s, sm_r,
):
    x, s, y = lax.axis_index("sec"), lax.axis_index("seq"), lax.axis_index("tp")
    z, c = s // 2, s % 2
    nseq = 2 * nz
    tok, feat = text.shape
    slots = img.shape[0]
    rows = tok + slots
    cols = cot.shape[1]
    halves = cols // LANES
    npos = 2 * nx * nseq
    half = feat // 2

    def remote(src, dst, ss, rs, dev):
        return pltpu.make_async_remote_copy(
            src_ref=src, dst_ref=dst, send_sem=ss, recv_sem=rs, device_id=dev, device_id_type=MESH
        )

    def loop(lo, hi, body):
        if hi > lo:
            lax.fori_loop(lo, hi, lambda i, t: (body(i), t)[1], 0)

    pairs = [(w_h, w), (ts_h, ts), (cot_h, cot), (sd_h, sd), (gain_h, gain), (text_h, text), (img_h, img)]
    fetch = [pltpu.make_async_copy(p, q, in_sem.at[i]) for i, (p, q) in enumerate(pairs)]
    for f in fetch:
        f.start()

    barrier = pltpu.get_barrier_semaphore()

    def greet(dev):
        pl.semaphore_signal(barrier, inc=1, device_id=dev, device_id_type=MESH)

    loop(1, nseq, lambda k: greet((x, lax.rem(s + k, nseq), y)))
    for k in range(1, nx):
        greet((lax.rem(x + k, nx), s, y))
    for k in range(1, ny):
        greet((x, s, lax.rem(y + k, ny)))

    def at_z(o):
        return lax.rem(z + (o + nz) % nz, nz)

    def at_x(o):
        return lax.rem(x + (o + nx) % nx, nx)

    sib = (x, s + 1 - 2 * c, y)

    def copy_z1(i):
        n = NEAR[i]
        own, got = wq.at[x, 0, c], wq.at[x, SLOT[n % 16], c]
        dev = (x, 2 * at_z(-n) + c, y)
        return Pair(
            lambda: remote(own, got, z1_s.at[i], z1_r.at[i], dev),
            lambda: remote(got, got, z1_s.at[i], z1_r.at[i], dev),
        )

    def copy_z2(e, i):
        n, m = NEAR[i], STEPS.index(e)
        out, got = wq.at[x, SLOT[n % 16], c], wq.at[x, SLOT[(n + e) % 16], c]
        dev = (x, 2 * at_z(-e) + c, y)
        return Pair(
            lambda: remote(out, got, z2_s.at[m, i], z2_r.at[m, i], dev),
            lambda: remote(got, got, z2_s.at[m, i], z2_r.at[m, i], dev),
        )

    def copy_z8(m):
        n, to = (5, -3) if m == 0 else (-5, 3)
        part = pl.ds(m * (half // 2), half // 2)
        out, got = wq.at[x, SLOT[n % 16], c, :, part], wq.at[x, SLOT[8], c, :, part]
        dev = (x, 2 * at_z(to) + c, y)
        return Pair(
            lambda: remote(out, got, z8_s.at[m], z8_r.at[m], dev),
            lambda: remote(got, got, z8_s.at[m], z8_r.at[m], dev),
        )

    def copy_x(j, m):
        up = m == 0 or (m == 2 and j % 2 == 0)
        frm = 0 if m < 2 else (-1 if up else 1)
        out = wq.at[at_x(frm), j, c]
        got = wq.at[at_x(frm + (-1 if up else 1)), j, c]
        dev = (at_x(1 if up else -1), s, y)
        return Pair(
            lambda: remote(out, out, x_s.at[j, m], x_r.at[j, m], dev),
            lambda: remote(got, got, x_s.at[j, m], x_r.at[j, m], dev),
        )

    def copy_sib(j):
        out, got = wq.at[:, j, c], wq.at[:, j, 1 - c]
        return Pair(
            lambda: remote(out, out, sib_s.at[j], sib_r.at[j], sib),
            lambda: remote(got, got, sib_s.at[j], sib_r.at[j], sib),
        )

    fetch[0].wait()
    w8 = w[...].astype(F32)
    wq[x, 0, c] = jnp.concatenate([w8[:, :half], w8[:, half:]], axis=0).astype(BF16)
    pl.semaphore_wait(barrier, nseq - 1 + nx - 1 + ny - 1)
    copy_z2(1, 0)[0].start()
    copy_z2(-1, 0)[0].start()
    copy_x(0, 0)[0].start()
    copy_x(0, 1)[0].start()
    for i in range(1, 3):
        copy_z1(i)[0].start()
    copy_z2(2, 0)[0].start()
    copy_z2(-2, 0)[0].start()

    def pick_rows(key):
        n = key.shape[1]
        return jnp.where(lax.broadcasted_iota(jnp.int32, (npos, n), 0).astype(F32) == key, 1.0, 0.0).astype(BF16)

    def pick_cols(pos):
        n = pos.shape[0]
        return jnp.where(lax.broadcasted_iota(jnp.int32, (n, npos), 1).astype(F32) == pos, 1.0, 0.0).astype(BF16)

    def fill1(key, values, b1, r1):
        g = jnp.dot(pick_rows(key), values, preferred_element_type=F32)
        parts = [g[:, h * LANES : (h + 1) * LANES].reshape(nseq, 2 * nx, LANES) for h in range(halves)]
        b1[...] = jnp.concatenate(parts, axis=1).astype(BF16)
        r1[s] = b1[s]

    def fill2(r1, b2, r2):
        r = r1[...].astype(F32)
        m = jnp.concatenate(
            [r[:, h * 2 * nx : (h + 1) * 2 * nx].reshape(npos, LANES) for h in range(halves)], axis=1
        ).astype(BF16)
        i = lax.broadcasted_iota(jnp.int32, (npos, npos), 0)
        j = lax.broadcasted_iota(jnp.int32, (npos, npos), 1)
        lx, ls = shift_of(2 * nseq), shift_of(nseq)
        i_x = lax.shift_right_arithmetic(i, jnp.full_like(i, lx))
        i_s = lax.shift_right_arithmetic(i, jnp.full_like(i, 1)) & (nseq - 1)
        perm = jnp.where((i_s * nx + i_x) * 2 + (i & 1) == j, 1.0, 0.0).astype(BF16)
        b2[...] = jnp.dot(perm, m, preferred_element_type=F32).astype(BF16).reshape(nx, 2 * nseq, cols)
        r2[x] = b2[x]

    def take(pos, r2):
        return jnp.dot(pick_cols(pos), r2[...].reshape(npos, cols), preferred_element_type=F32)

    def copy1(n, b1, r1, k):
        to, frm = lax.rem(s + k, nseq), lax.rem(s + nseq - k, nseq)
        return Pair(
            lambda: remote(b1.at[to], r1.at[s], e1_s.at[n, k], e1_r.at[n, k], (x, to, y)),
            lambda: remote(b1.at[to], r1.at[frm], e1_s.at[n, k], e1_r.at[n, k], (x, to, y)),
        )

    def copy2(n, b2, r2, k):
        to, frm = lax.rem(x + k, nx), lax.rem(x + nx - k, nx)
        return Pair(
            lambda: remote(b2.at[to], r2.at[x], e2_s.at[n, k], e2_r.at[n, k], (to, s, y)),
            lambda: remote(b2.at[to], r2.at[frm], e2_s.at[n, k], e2_r.at[n, k], (to, s, y)),
        )

    def copy_y(part, k):
        to, frm = lax.rem(y + k, ny), lax.rem(y + ny - k, ny)
        at = pl.ds(0, tok) if part == 0 else pl.ds(tok, slots)
        return Pair(
            lambda: remote(cots.at[y, at], cots.at[y, at], yc_s.at[part, k], yc_r.at[part, k], (x, s, to)),
            lambda: remote(cots.at[y, at], cots.at[frm, at], yc_s.at[part, k], yc_r.at[part, k], (x, s, to)),
        )

    def copy_rs(grp, part, k):
        at = pl.ds(0, tok) if part == 0 else pl.ds(tok, slots)
        to = lax.rem(y + k, ny)
        return remote(
            rs_send.at[grp, k, at], rs_recv.at[grp, k, at], rs_s.at[grp, part, k], rs_r.at[grp, part, k], (x, s, to)
        )

    def copy_sum(n, k):
        to = lax.rem(y + k, ny)
        return remote(sum_send.at[n], sum_recv.at[n, k], sm_s.at[n, k], sm_r.at[n, k], (x, s, to))

    p = lax.broadcasted_iota(jnp.int32, (1, cols), 1)
    up_by = jnp.zeros_like(p)
    for j, (n, _) in enumerate(ORDER):
        up_by = jnp.where(lax.shift_right_arithmetic(p, jnp.full_like(p, 4)) == j, n + nz, up_by)
    place_of = ((z + up_by) & (nz - 1)) * 16 + (p & 15)
    reorder = jnp.where(lax.broadcasted_iota(jnp.int32, (cols, cols), 0) == place_of, 1.0, 0.0).astype(BF16)

    def to_pieces(v):
        return jnp.dot(v, reorder, preferred_element_type=F32).astype(BF16)

    def to_columns(v):
        return lax.dot_general(v, reorder, (((1,), (1,)), ((), ())), preferred_element_type=F32).astype(BF16)

    fetch[1].wait()
    fetch[2].wait()
    key_tok, pos_tok, own_tok = places(ts[...], shift_of(slots), nx, nseq)
    fill1(key_tok, cot[...], b1a, r1a)
    cots[y, :tok] = to_pieces(cot[...])

    def prepare(ref, base, lo, hi):
        def body(i):
            r = ref[pl.ds(pl.multiple_of(i * 16, 16), 16), :].astype(F32)
            at = pl.ds(pl.multiple_of(base + i * 16, 16), 16)
            xg[at, :] = (r * gain[...]).astype(BF16)
            sq[at, :] = jnp.broadcast_to(jnp.sum(r * r, axis=1, keepdims=True), (16, LANES))

        loop(lo, hi, body)

    work = {}
    for n in range(4):
        b = tok // 64
        work[9 + n] = [functools.partial(prepare, text, 0, n * b, (n + 1) * b)]
    for n in range(2):
        b = slots // 32
        work[13 + n] = [functools.partial(prepare, img, tok, n * b, (n + 1) * b)]

    def send_squares():
        sum_send[0] = jnp.transpose(sq[...])[:8]
        for k in range(1, ny):
            copy_sum(0, k).start()

    work[15] = [send_squares]

    def middle():
        loop(1, nseq, lambda k: copy1(0, b1a, r1a, k)[1].wait_recv())
        fill2(r1a, b2a, r2a)
        for k in range(1, nx):
            copy2(0, b2a, r2a, k)[0].start()

    work[19] = [middle]
    work[21] = [lambda: loop(1, nseq, lambda k: copy1(0, b1a, r1a, k)[0].wait_send())]
    keys = []

    def slot_cots():
        for k in range(1, nx):
            copy2(0, b2a, r2a, k)[1].wait_recv()
        cots[y, tok:] = to_pieces(take(keys[0][1], r2a).astype(BF16))
        for k in range(1, ny):
            copy_y(1, k)[0].start()


    def weights(t, grp, h):
        lo, hi = (0, nz) if grp is None else (grp * (nz // 2), (grp + 1) * (nz // 2))
        return wq[t, lo:hi, :, 8 * h : 8 * h + 8, :].reshape(16 * (hi - lo), half)

    def forward(grp):
        for j in range(grp * (nz // 2), (grp + 1) * (nz // 2)):
            copy_sib(j)[1].wait_recv()
        lanes = slice(grp * LANES, (grp + 1) * LANES)
        for part in (1, 0):
            lo, hi = (0, tok) if part == 0 else (tok, rows)
            v = jnp.zeros((hi - lo, ny * LANES), F32)
            for h in range(2):
                rhs = jnp.concatenate([weights(lax.rem(y + k, ny), grp, h) for k in range(ny)], axis=0)
                v = v + lax.dot_general(
                    xg[lo:hi, h * half : (h + 1) * half], rhs, (((1,), (1,)), ((), ())), preferred_element_type=F32
                )
            for k in (2, 1, 3, 0):
                u = v[:, k * LANES : (k + 1) * LANES]
                if k:
                    rs_send[grp, k, lo:hi] = u.astype(BF16)
                    if (grp, part) != (1, 0):
                        copy_rs(grp, part, k).start()
                else:
                    kvp[lo:hi, lanes] = u
                vs[grp, k, lo:hi] = u

    def sent_z():
        for i in range(1, 3):
            copy_z1(i)[0].wait_send()
        for i in range(3):
            for e in STEPS:
                copy_z2(e, i)[0].wait_send()
        for m in range(2):
            copy_z8(m)[0].wait_send()

    pieces = len(ORDER)
    work.setdefault(pieces + LAG1 - 1, []).append(functools.partial(forward, 0))
    for j in range(pieces + LAG2):
        if 1 <= j < pieces:
            come = ORDER[j][1]
            if come is None:
                copy_z8(0)[1].wait_recv()
                copy_z8(1)[1].wait_recv()
            elif come[0]:
                copy_z2(*come)[1].wait_recv()
            else:
                i = come[1]
                copy_z1(i)[1].wait_recv()
                for e in STEPS:
                    copy_z2(e, i)[0].start()
                copy_z8(i - 1)[0].start()
            copy_x(j, 0)[0].start()
            copy_x(j, 1)[0].start()
        if j == 8:
            for k in range(1, ny):
                copy_y(0, k)[0].start()
        if j == EXCH:
            loop(1, nseq, lambda k: copy1(0, b1a, r1a, k)[0].start())
        if LAG1 <= j < pieces + LAG1:
            i = j - LAG1
            copy_x(i, 0)[1].wait_recv()
            copy_x(i, 1)[1].wait_recv()
            copy_x(i, 2)[0].start()
        if LAG2 <= j:
            copy_x(j - LAG2, 2)[1].wait_recv()
            copy_sib(j - LAG2)[0].start()
            for m in range(2):
                copy_x(j - LAG2, m)[0].wait_send()
        if j == pieces:
            sent_z()
        if j == 1:
            for f in fetch[3:]:
                f.wait()
        for f in work.get(j, ()):
            f()

    total = sum_send[0]
    for k in range(1, ny):
        copy_sum(0, k).wait_recv()
        total = total + sum_recv[0, k]
    scale_r = lax.rsqrt(total[0:1] / D + EPS)
    sq[...] = jnp.transpose(jnp.broadcast_to(scale_r, (LANES, rows)))
    forward(1)
    keys.append(places(sd[...], shift_of(tok), nx, nseq))
    key_slot, pos_slot, own_slot = keys[0]

    def reduced(part):
        lo, hi = (0, tok) if part == 0 else (tok, rows)
        raw = kvp[lo:hi]
        for k in range(1, ny):
            for grp in range(2):
                copy_rs(grp, part, k).wait_recv()
            raw = raw + jnp.concatenate([rs_recv[0, k, lo:hi], rs_recv[1, k, lo:hi]], axis=1).astype(F32)
        return to_columns((raw * sq[lo:hi, 0:1]).astype(BF16))

    fill1(key_slot, reduced(1), b1b, r1b)
    for k in range(1, nseq):
        copy1(1, b1b, r1b, k)[0].start()
    slot_cots()
    for k in (2, 1, 3):
        copy_rs(1, 0, k).start()

    def backward(lo, hi):
        cot_all = jnp.concatenate([cots[t, lo:hi] for t in range(ny)], axis=1)
        for h in range(2):
            rhs = jnp.concatenate([weights(t, None, h) for t in range(ny)], axis=0)
            acc[lo:hi, h * half : (h + 1) * half] = jnp.dot(cot_all, rhs, preferred_element_type=F32)

    for k in range(1, ny):
        copy_y(0, k)[1].wait_recv()
    backward(0, tok)
    for k in range(1, ny):
        copy_y(1, k)[1].wait_recv()
    dots = jnp.zeros((rows, LANES), F32)
    for k in range(ny):
        near = cots[lax.rem(y + k, ny)].astype(F32)
        for grp in range(2):
            dots = dots + vs[grp, k] * near[:, grp * LANES : (grp + 1) * LANES]
    sum_send[1] = jnp.transpose(jnp.broadcast_to(jnp.sum(dots, axis=1, keepdims=True), (rows, LANES)))[:8]
    for k in range(1, ny):
        copy_sum(1, k).start()
    backward(tok, rows)

    total = sum_send[1]
    for k in range(1, ny):
        copy_sum(1, k).wait_recv()
        total = total + sum_recv[1, k]
    coef_r = scale_r * scale_r * scale_r * total[0:1] / D
    coef = jnp.transpose(jnp.broadcast_to(coef_r, (LANES, rows)))
    keep = jnp.concatenate([jnp.where(own_tok < 0.0, 1.0, 0.0), jnp.where(own_slot >= 0.0, 1.0, 0.0)], axis=0)
    lane = lax.broadcasted_iota(jnp.int32, (rows, LANES), 1)
    sq[...] = jnp.where(lane == 0, sq[...], jnp.where(lane == 1, coef, keep))

    results = ((tg_out, tg_h), (ig_out, ig_h), (kv_out, kv_h))
    done = [pltpu.make_async_copy(p, q, out_sem.at[i]) for i, (p, q) in enumerate(results)]

    def grads(ref, base, out):
        def body(i):
            here = pl.ds(pl.multiple_of(i * 16, 16), 16)
            at = pl.ds(pl.multiple_of(base + i * 16, 16), 16)
            r = ref[here, :].astype(F32)
            f = sq[at, :]
            g = f[:, 0:1] * (gain[...] * acc[at, :]) - r * f[:, 1:2]
            out[here, :] = jnp.where(f[:, 2:3] > 0.0, g, 0.0).astype(BF16)

        loop(0, ref.shape[0] // 16, body)

    loop(1, nseq, lambda k: copy1(1, b1b, r1b, k)[1].wait_recv())
    fill2(r1b, b2b, r2b)
    for k in range(1, nx):
        copy2(1, b2b, r2b, k)[0].start()
    grads(text, 0, tg_out)
    done[0].start()
    grads(img, tok, ig_out)
    done[1].start()
    kv_text = reduced(0)
    for j in range(pieces):
        copy_x(j, 2)[0].wait_send()
        copy_sib(j)[0].wait_send()
    for k in range(1, nx):
        copy2(0, b2a, r2a, k)[0].wait_send()
    for k in range(1, ny):
        for part in range(2):
            copy_y(part, k)[0].wait_send()
            copy_rs(0, part, k).wait_send()
            copy_rs(1, part, k).wait_send()
            copy_sum(part, k).wait_send()

    def sent1(k):
        copy1(1, b1b, r1b, k)[0].wait_send()

    loop(1, nseq, sent1)

    for k in range(1, nx):
        copy2(1, b2b, r2b, k)[1].wait_recv()
    got = take(pos_tok, r2b)
    kv_out[...] = jnp.where(own_tok >= 0.0, got, kv_text.astype(F32)).astype(BF16)
    done[2].start()
    for d in done:
        d.wait()
    for k in range(1, nx):
        copy2(1, b2b, r2b, k)[0].wait_send()


def flush(a, b, c, out_a, out_b, out_c, via_a, via_b, via_c, sem):
    ways = ((b, via_b, out_b), (c, via_c, out_c), (a, via_a, out_a))
    into = [pltpu.make_async_copy(p, v, sem.at[0, i]) for i, (p, v, _) in enumerate(ways)]
    away = [pltpu.make_async_copy(v, q, sem.at[1, i]) for i, (_, v, q) in enumerate(ways)]
    for p in into:
        p.start()
    for p, q in zip(into, away):
        p.wait()
        q.start()
    for q in away:
        q.wait()


def per_device(text_embed, image_rows, token_source, slot_dest, norm_gain, kv_weight, kv_cot):
    nx, nseq, ny = lax.axis_size("sec"), lax.axis_size("seq"), lax.axis_size("tp")
    nz = nseq // 2
    tok, feat = text_embed.shape
    slots = image_rows.shape[0]
    rows = tok + slots
    cols = kv_cot.shape[1]
    dma = pltpu.SemaphoreType.DMA
    blk = (2 * nx * cols) // LANES
    exch = [
        pltpu.VMEM((nseq, blk, LANES), BF16),
        pltpu.VMEM((nseq, blk, LANES), BF16),
        pltpu.VMEM((nx, 2 * nseq, cols), BF16),
        pltpu.VMEM((nx, 2 * nseq, cols), BF16),
    ]
    hbm = pl.BlockSpec(memory_space=pl.ANY)
    outs = pl.pallas_call(
        functools.partial(kernel, nx, nz, ny),
        out_shape=(
            jax.ShapeDtypeStruct((tok, cols), BF16),
            jax.ShapeDtypeStruct((tok, feat), BF16),
            jax.ShapeDtypeStruct((slots, feat), BF16),
        ),
        in_specs=[pl.BlockSpec(memory_space=pl.ANY)] * 7,
        out_specs=(hbm, hbm, hbm),
        scratch_shapes=[
            pltpu.VMEM((tok, cols), BF16),
            pltpu.VMEM((tok, feat), BF16),
            pltpu.VMEM((slots, feat), BF16),
            pltpu.VMEM((tok, feat), BF16),
            pltpu.VMEM((slots, feat), BF16),
            pltpu.VMEM((1, tok), jnp.int32),
            pltpu.VMEM((1, slots), jnp.int32),
            pltpu.VMEM((1, feat), F32),
            pltpu.VMEM((8, feat), BF16),
            pltpu.VMEM((tok, cols), BF16),
            pltpu.VMEM((nx, nz, 2, 16, feat // 2), BF16),
            pltpu.VMEM((rows, feat), BF16),
            pltpu.VMEM((ny, rows, cols), BF16),
            pltpu.VMEM((rows, LANES), F32),
            pltpu.VMEM((rows, feat), F32),
            pltpu.VMEM((2, ny, rows, LANES), F32),
            pltpu.VMEM((rows, cols), F32),
            pltpu.VMEM((2, ny, rows, LANES), BF16),
            pltpu.VMEM((2, ny, rows, LANES), BF16),
            pltpu.VMEM((2, 8, rows), F32),
            pltpu.VMEM((2, ny, 8, rows), F32),
            *exch,
            *exch,
            dma((3,)),
            dma((7,)),
            *[dma((3,))] * 2,
            *[dma((4, 3))] * 2,
            *[dma((2,))] * 2,
            *[dma((nz, 3))] * 2,
            *[dma((nz,))] * 2,
            *[dma((2, nseq))] * 2,
            *[dma((2, nx))] * 2,
            *[dma((2, ny))] * 2,
            *[dma((2, 2, ny))] * 2,
            *[dma((2, ny))] * 2,
        ],
        compiler_params=pltpu.CompilerParams(
            collective_id=0, has_side_effects=True, vmem_limit_bytes=58 * 2**20
        ),
        cost_estimate=pl.CostEstimate(
            flops=4 * rows * feat * cols * ny, bytes_accessed=8 * rows * feat, transcendentals=0
        ),
    )(
        text_embed,
        image_rows,
        token_source.reshape(1, tok),
        slot_dest.reshape(1, slots),
        norm_gain.reshape(1, feat),
        kv_weight,
        kv_cot,
    )
    where = pl.BlockSpec(memory_space=pl.ANY)
    return pl.pallas_call(
        flush,
        out_shape=tuple(jax.ShapeDtypeStruct(o.shape, o.dtype) for o in outs),
        in_specs=[where] * 3,
        out_specs=(where,) * 3,
        scratch_shapes=[*[pltpu.VMEM(o.shape, o.dtype) for o in outs], dma((2, 3))],
        compiler_params=pltpu.CompilerParams(vmem_limit_bytes=58 * 2**20),
    )(*outs)


def solution(mesh):
    both = P(("sec", "seq"), "tp")
    rows = P(("sec", "seq"))
    return jax.shard_map(
        per_device,
        mesh=mesh,
        in_specs=(both, both, rows, rows, P("tp"), both, both),
        out_specs=(both, both, both),
        check_vma=False,
    )
```

```python
import functools

import jax
import jax.numpy as jnp
from jax import lax
from jax.experimental import pallas as pl
from jax.experimental.pallas import tpu as pltpu
from jax.sharding import PartitionSpec as P

D = 8192
EPS = 1e-06
F32 = jnp.float32
BF16 = jnp.bfloat16
MESH = pl.DeviceIdType.MESH
LANES = 128


class Pair:
    def __init__(self, out, into):
        self.ends = (out, into)

    def __getitem__(self, i):
        return self.ends[i]()


def shift_of(n):
    return n.bit_length() - 1


def places(row, log_owner, nx, nseq):
    n = row.shape[1]
    own = lax.shift_right_arithmetic(row, jnp.full_like(row, log_owner))
    own_row = own.astype(F32)
    ii = lax.broadcasted_iota(jnp.int32, (n, n), 0)
    jj = lax.broadcasted_iota(jnp.int32, (n, n), 1)
    own_col = jnp.sum(jnp.where(ii == jj, own_row, 0.0), axis=1, keepdims=True)
    eq = own_col == own_row
    rank_row = jnp.sum(jnp.where(eq & (ii < jj), 1.0, 0.0), axis=0, keepdims=True)
    rank_col = jnp.sum(jnp.where(eq & (jj < ii), 1.0, 0.0), axis=1, keepdims=True)
    x_of = lax.shift_right_arithmetic(own, jnp.full_like(own, shift_of(nseq)))
    s_of = own & (nseq - 1)
    key = ((s_of * nx + x_of) * 2).astype(F32) + rank_row
    key = jnp.where(own_row >= 0.0, key, -1.0)
    pos = jnp.where(own_col >= 0.0, own_col * 2.0 + rank_col, -1.0)
    return key, pos, own_col


NEAR = (0, 5, -5)
STEPS = (1, -1, 2, -2)
ORDER = (
    [(0, (0, 0))]
    + [(e, (e, 0)) for e in STEPS]
    + [(NEAR[i], (0, i)) for i in (1, 2)]
    + [(NEAR[i] + e, (e, i)) for e in STEPS for i in (1, 2)]
    + [(8, None)]
)
LAG1, LAG2, EXCH = 3, 7, 12
SLOT = {(n + 16) % 16: j for j, (n, _) in enumerate(ORDER)}


def kernel(
    nx, nz, ny,
    text_h, img_h, ts_h, sd_h, gain_h, w_h, cot_h,
    kv_h, tg_h, ig_h,
    kv_out, tg_out, ig_out,
    text, img, ts, sd, gain, w, cot,
    wq, xg, cots, sq, acc, vs, kvp, rs_send, rs_recv, sum_send, sum_recv,
    b1a, r1a, b2a, r2a, b1b, r1b, b2b, r2b,
    out_sem, in_sem, z1_s, z1_r, z2_s, z2_r, z8_s, z8_r, x_s, x_r, sib_s, sib_r,
    e1_s, e1_r, e2_s, e2_r, yc_s, yc_r, rs_s, rs_r, sm_s, sm_r,
):
    x, s, y = lax.axis_index("sec"), lax.axis_index("seq"), lax.axis_index("tp")
    z, c = s // 2, s % 2
    nseq = 2 * nz
    tok, feat = text.shape
    slots = img.shape[0]
    rows = tok + slots
    cols = cot.shape[1]
    halves = cols // LANES
    npos = 2 * nx * nseq
    half = feat // 2

    def remote(src, dst, ss, rs, dev):
        return pltpu.make_async_remote_copy(
            src_ref=src, dst_ref=dst, send_sem=ss, recv_sem=rs, device_id=dev, device_id_type=MESH
        )

    def loop(lo, hi, body):
        if hi > lo:
            lax.fori_loop(lo, hi, lambda i, t: (body(i), t)[1], 0)

    pairs = [(w_h, w), (ts_h, ts), (cot_h, cot), (sd_h, sd), (gain_h, gain), (text_h, text), (img_h, img)]
    fetch = [pltpu.make_async_copy(p, q, in_sem.at[i]) for i, (p, q) in enumerate(pairs)]
    for f in fetch:
        f.start()

    barrier = pltpu.get_barrier_semaphore()

    def greet(dev):
        pl.semaphore_signal(barrier, inc=1, device_id=dev, device_id_type=MESH)

    loop(1, nseq, lambda k: greet((x, lax.rem(s + k, nseq), y)))
    for k in range(1, nx):
        greet((lax.rem(x + k, nx), s, y))
    for k in range(1, ny):
        greet((x, s, lax.rem(y + k, ny)))

    def at_z(o):
        return lax.rem(z + (o + nz) % nz, nz)

    def at_x(o):
        return lax.rem(x + (o + nx) % nx, nx)

    sib = (x, s + 1 - 2 * c, y)

    def copy_z1(i):
        n = NEAR[i]
        own, got = wq.at[x, 0, c], wq.at[x, SLOT[n % 16], c]
        dev = (x, 2 * at_z(-n) + c, y)
        return Pair(
            lambda: remote(own, got, z1_s.at[i], z1_r.at[i], dev),
            lambda: remote(got, got, z1_s.at[i], z1_r.at[i], dev),
        )

    def copy_z2(e, i):
        n, m = NEAR[i], STEPS.index(e)
        out, got = wq.at[x, SLOT[n % 16], c], wq.at[x, SLOT[(n + e) % 16], c]
        dev = (x, 2 * at_z(-e) + c, y)
        return Pair(
            lambda: remote(out, got, z2_s.at[m, i], z2_r.at[m, i], dev),
            lambda: remote(got, got, z2_s.at[m, i], z2_r.at[m, i], dev),
        )

    def copy_z8(m):
        n, to = (5, -3) if m == 0 else (-5, 3)
        part = pl.ds(m * (half // 2), half // 2)
        out, got = wq.at[x, SLOT[n % 16], c, :, part], wq.at[x, SLOT[8], c, :, part]
        dev = (x, 2 * at_z(to) + c, y)
        return Pair(
            lambda: remote(out, got, z8_s.at[m], z8_r.at[m], dev),
            lambda: remote(got, got, z8_s.at[m], z8_r.at[m], dev),
        )

    def copy_x(j, m):
        up = m == 0 or (m == 2 and j % 2 == 0)
        frm = 0 if m < 2 else (-1 if up else 1)
        out = wq.at[at_x(frm), j, c]
        got = wq.at[at_x(frm + (-1 if up else 1)), j, c]
        dev = (at_x(1 if up else -1), s, y)
        return Pair(
            lambda: remote(out, out, x_s.at[j, m], x_r.at[j, m], dev),
            lambda: remote(got, got, x_s.at[j, m], x_r.at[j, m], dev),
        )

    def copy_sib(j):
        out, got = wq.at[:, j, c], wq.at[:, j, 1 - c]
        return Pair(
            lambda: remote(out, out, sib_s.at[j], sib_r.at[j], sib),
            lambda: remote(got, got, sib_s.at[j], sib_r.at[j], sib),
        )

    fetch[0].wait()
    w8 = w[...].astype(F32)
    wq[x, 0, c] = jnp.concatenate([w8[:, :half], w8[:, half:]], axis=0).astype(BF16)
    pl.semaphore_wait(barrier, nseq - 1 + nx - 1 + ny - 1)
    copy_z2(1, 0)[0].start()
    copy_z2(-1, 0)[0].start()
    copy_x(0, 0)[0].start()
    copy_x(0, 1)[0].start()
    for i in range(1, 3):
        copy_z1(i)[0].start()
    copy_z2(2, 0)[0].start()
    copy_z2(-2, 0)[0].start()

    def pick_rows(key):
        n = key.shape[1]
        return jnp.where(lax.broadcasted_iota(jnp.int32, (npos, n), 0).astype(F32) == key, 1.0, 0.0).astype(BF16)

    def pick_cols(pos):
        n = pos.shape[0]
        return jnp.where(lax.broadcasted_iota(jnp.int32, (n, npos), 1).astype(F32) == pos, 1.0, 0.0).astype(BF16)

    def fill1(key, values, b1, r1):
        g = jnp.dot(pick_rows(key), values, preferred_element_type=F32)
        parts = [g[:, h * LANES : (h + 1) * LANES].reshape(nseq, 2 * nx, LANES) for h in range(halves)]
        b1[...] = jnp.concatenate(parts, axis=1).astype(BF16)
        r1[s] = b1[s]

    def fill2(r1, b2, r2):
        r = r1[...].astype(F32)
        m = jnp.concatenate(
            [r[:, h * 2 * nx : (h + 1) * 2 * nx].reshape(npos, LANES) for h in range(halves)], axis=1
        ).astype(BF16)
        i = lax.broadcasted_iota(jnp.int32, (npos, npos), 0)
        j = lax.broadcasted_iota(jnp.int32, (npos, npos), 1)
        lx, ls = shift_of(2 * nseq), shift_of(nseq)
        i_x = lax.shift_right_arithmetic(i, jnp.full_like(i, lx))
        i_s = lax.shift_right_arithmetic(i, jnp.full_like(i, 1)) & (nseq - 1)
        perm = jnp.where((i_s * nx + i_x) * 2 + (i & 1) == j, 1.0, 0.0).astype(BF16)
        b2[...] = jnp.dot(perm, m, preferred_element_type=F32).astype(BF16).reshape(nx, 2 * nseq, cols)
        r2[x] = b2[x]

    def take(pos, r2):
        return jnp.dot(pick_cols(pos), r2[...].reshape(npos, cols), preferred_element_type=F32)

    def copy1(n, b1, r1, k):
        to, frm = lax.rem(s + k, nseq), lax.rem(s + nseq - k, nseq)
        return Pair(
            lambda: remote(b1.at[to], r1.at[s], e1_s.at[n, k], e1_r.at[n, k], (x, to, y)),
            lambda: remote(b1.at[to], r1.at[frm], e1_s.at[n, k], e1_r.at[n, k], (x, to, y)),
        )

    def copy2(n, b2, r2, k):
        to, frm = lax.rem(x + k, nx), lax.rem(x + nx - k, nx)
        return Pair(
            lambda: remote(b2.at[to], r2.at[x], e2_s.at[n, k], e2_r.at[n, k], (to, s, y)),
            lambda: remote(b2.at[to], r2.at[frm], e2_s.at[n, k], e2_r.at[n, k], (to, s, y)),
        )

    def copy_y(part, k):
        to, frm = lax.rem(y + k, ny), lax.rem(y + ny - k, ny)
        at = pl.ds(0, tok) if part == 0 else pl.ds(tok, slots)
        return Pair(
            lambda: remote(cots.at[y, at], cots.at[y, at], yc_s.at[part, k], yc_r.at[part, k], (x, s, to)),
            lambda: remote(cots.at[y, at], cots.at[frm, at], yc_s.at[part, k], yc_r.at[part, k], (x, s, to)),
        )

    def copy_rs(grp, part, k):
        at = pl.ds(0, tok) if part == 0 else pl.ds(tok, slots)
        to = lax.rem(y + k, ny)
        return remote(
            rs_send.at[grp, k, at], rs_recv.at[grp, k, at], rs_s.at[grp, part, k], rs_r.at[grp, part, k], (x, s, to)
        )

    def copy_sum(n, k):
        to = lax.rem(y + k, ny)
        return remote(sum_send.at[n], sum_recv.at[n, k], sm_s.at[n, k], sm_r.at[n, k], (x, s, to))

    p = lax.broadcasted_iota(jnp.int32, (1, cols), 1)
    up_by = jnp.zeros_like(p)
    for j, (n, _) in enumerate(ORDER):
        up_by = jnp.where(lax.shift_right_arithmetic(p, jnp.full_like(p, 4)) == j, n + nz, up_by)
    place_of = ((z + up_by) & (nz - 1)) * 16 + (p & 15)
    reorder = jnp.where(lax.broadcasted_iota(jnp.int32, (cols, cols), 0) == place_of, 1.0, 0.0).astype(BF16)

    def to_pieces(v):
        return jnp.dot(v, reorder, preferred_element_type=F32).astype(BF16)

    def to_columns(v):
        return lax.dot_general(v, reorder, (((1,), (1,)), ((), ())), preferred_element_type=F32).astype(BF16)

    fetch[1].wait()
    fetch[2].wait()
    key_tok, pos_tok, own_tok = places(ts[...], shift_of(slots), nx, nseq)
    fill1(key_tok, cot[...], b1a, r1a)
    cots[y, :tok] = to_pieces(cot[...])

    def prepare(ref, base, lo, hi):
        def body(i):
            r = ref[pl.ds(pl.multiple_of(i * 16, 16), 16), :].astype(F32)
            at = pl.ds(pl.multiple_of(base + i * 16, 16), 16)
            xg[at, :] = (r * gain[...]).astype(BF16)
            sq[at, :] = jnp.broadcast_to(jnp.sum(r * r, axis=1, keepdims=True), (16, LANES))

        loop(lo, hi, body)

    work = {}
    for n in range(4):
        b = tok // 64
        work[9 + n] = [functools.partial(prepare, text, 0, n * b, (n + 1) * b)]
    for n in range(2):
        b = slots // 32
        work[13 + n] = [functools.partial(prepare, img, tok, n * b, (n + 1) * b)]

    def send_squares():
        sum_send[0] = jnp.transpose(sq[...])[:8]
        for k in range(1, ny):
            copy_sum(0, k).start()

    work[15] = [send_squares]

    def middle():
        loop(1, nseq, lambda k: copy1(0, b1a, r1a, k)[1].wait_recv())
        fill2(r1a, b2a, r2a)
        for k in range(1, nx):
            copy2(0, b2a, r2a, k)[0].start()

    work[19] = [middle]
    work[21] = [lambda: loop(1, nseq, lambda k: copy1(0, b1a, r1a, k)[0].wait_send())]
    keys = []

    def slot_cots():
        for k in range(1, nx):
            copy2(0, b2a, r2a, k)[1].wait_recv()
        cots[y, tok:] = to_pieces(take(keys[0][1], r2a).astype(BF16))
        for k in range(1, ny):
            copy_y(1, k)[0].start()


    def weights(t, grp, h):
        lo, hi = (0, nz) if grp is None else (grp * (nz // 2), (grp + 1) * (nz // 2))
        return wq[t, lo:hi, :, 8 * h : 8 * h + 8, :].reshape(16 * (hi - lo), half)

    def forward(grp):
        for j in range(grp * (nz // 2), (grp + 1) * (nz // 2)):
            copy_sib(j)[1].wait_recv()
        lanes = slice(grp * LANES, (grp + 1) * LANES)
        for part in (1, 0):
            lo, hi = (0, tok) if part == 0 else (tok, rows)
            v = jnp.zeros((hi - lo, ny * LANES), F32)
            for h in range(2):
                rhs = jnp.concatenate([weights(lax.rem(y + k, ny), grp, h) for k in range(ny)], axis=0)
                v = v + lax.dot_general(
                    xg[lo:hi, h * half : (h + 1) * half], rhs, (((1,), (1,)), ((), ())), preferred_element_type=F32
                )
            for k in (2, 1, 3, 0):
                u = v[:, k * LANES : (k + 1) * LANES]
                if k:
                    rs_send[grp, k, lo:hi] = u.astype(BF16)
                    if (grp, part) != (1, 0):
                        copy_rs(grp, part, k).start()
                else:
                    kvp[lo:hi, lanes] = u
                vs[grp, k, lo:hi] = u

    def sent_z():
        for i in range(1, 3):
            copy_z1(i)[0].wait_send()
        for i in range(3):
            for e in STEPS:
                copy_z2(e, i)[0].wait_send()
        for m in range(2):
            copy_z8(m)[0].wait_send()

    pieces = len(ORDER)
    work.setdefault(pieces + LAG1 - 1, []).append(functools.partial(forward, 0))
    for j in range(pieces + LAG2):
        if 1 <= j < pieces:
            come = ORDER[j][1]
            if come is None:
                copy_z8(0)[1].wait_recv()
                copy_z8(1)[1].wait_recv()
            elif come[0]:
                copy_z2(*come)[1].wait_recv()
            else:
                i = come[1]
                copy_z1(i)[1].wait_recv()
                for e in STEPS:
                    copy_z2(e, i)[0].start()
                copy_z8(i - 1)[0].start()
            copy_x(j, 0)[0].start()
            copy_x(j, 1)[0].start()
        if j == 8:
            for k in range(1, ny):
                copy_y(0, k)[0].start()
        if j == EXCH:
            loop(1, nseq, lambda k: copy1(0, b1a, r1a, k)[0].start())
        if LAG1 <= j < pieces + LAG1:
            i = j - LAG1
            copy_x(i, 0)[1].wait_recv()
            copy_x(i, 1)[1].wait_recv()
            copy_x(i, 2)[0].start()
        if LAG2 <= j:
            copy_x(j - LAG2, 2)[1].wait_recv()
            copy_sib(j - LAG2)[0].start()
            for m in range(2):
                copy_x(j - LAG2, m)[0].wait_send()
        if j == pieces:
            sent_z()
        if j == 1:
            for f in fetch[3:]:
                f.wait()
        for f in work.get(j, ()):
            f()

    total = sum_send[0]
    for k in range(1, ny):
        copy_sum(0, k).wait_recv()
        total = total + sum_recv[0, k]
    scale_r = lax.rsqrt(total[0:1] / D + EPS)
    sq[...] = jnp.transpose(jnp.broadcast_to(scale_r, (LANES, rows)))
    forward(1)
    keys.append(places(sd[...], shift_of(tok), nx, nseq))
    key_slot, pos_slot, own_slot = keys[0]

    def reduced(part):
        lo, hi = (0, tok) if part == 0 else (tok, rows)
        raw = kvp[lo:hi]
        for k in range(1, ny):
            for grp in range(2):
                copy_rs(grp, part, k).wait_recv()
            raw = raw + jnp.concatenate([rs_recv[0, k, lo:hi], rs_recv[1, k, lo:hi]], axis=1).astype(F32)
        return to_columns((raw * sq[lo:hi, 0:1]).astype(BF16))

    fill1(key_slot, reduced(1), b1b, r1b)
    for k in range(1, nseq):
        copy1(1, b1b, r1b, k)[0].start()
    slot_cots()
    for k in (2, 1, 3):
        copy_rs(1, 0, k).start()

    def backward(lo, hi):
        cot_all = jnp.concatenate([cots[t, lo:hi] for t in range(ny)], axis=1)
        for h in range(2):
            rhs = jnp.concatenate([weights(t, None, h) for t in range(ny)], axis=0)
            acc[lo:hi, h * half : (h + 1) * half] = jnp.dot(cot_all, rhs, preferred_element_type=F32)

    for k in range(1, ny):
        copy_y(0, k)[1].wait_recv()
    backward(0, tok)
    for k in range(1, ny):
        copy_y(1, k)[1].wait_recv()
    dots = jnp.zeros((rows, LANES), F32)
    for k in range(ny):
        near = cots[lax.rem(y + k, ny)].astype(F32)
        for grp in range(2):
            dots = dots + vs[grp, k] * near[:, grp * LANES : (grp + 1) * LANES]
    sum_send[1] = jnp.transpose(jnp.broadcast_to(jnp.sum(dots, axis=1, keepdims=True), (rows, LANES)))[:8]
    for k in range(1, ny):
        copy_sum(1, k).start()
    backward(tok, rows)

    total = sum_send[1]
    for k in range(1, ny):
        copy_sum(1, k).wait_recv()
        total = total + sum_recv[1, k]
    coef_r = scale_r * scale_r * scale_r * total[0:1] / D
    coef = jnp.transpose(jnp.broadcast_to(coef_r, (LANES, rows)))
    keep = jnp.concatenate([jnp.where(own_tok < 0.0, 1.0, 0.0), jnp.where(own_slot >= 0.0, 1.0, 0.0)], axis=0)
    lane = lax.broadcasted_iota(jnp.int32, (rows, LANES), 1)
    sq[...] = jnp.where(lane == 0, sq[...], jnp.where(lane == 1, coef, keep))

    results = ((tg_out, tg_h), (ig_out, ig_h), (kv_out, kv_h))
    done = [pltpu.make_async_copy(p, q, out_sem.at[i]) for i, (p, q) in enumerate(results)]

    def grads(ref, base, out):
        def body(i):
            here = pl.ds(pl.multiple_of(i * 16, 16), 16)
            at = pl.ds(pl.multiple_of(base + i * 16, 16), 16)
            r = ref[here, :].astype(F32)
            f = sq[at, :]
            g = f[:, 0:1] * (gain[...] * acc[at, :]) - r * f[:, 1:2]
            out[here, :] = jnp.where(f[:, 2:3] > 0.0, g, 0.0).astype(BF16)

        loop(0, ref.shape[0] // 16, body)

    loop(1, nseq, lambda k: copy1(1, b1b, r1b, k)[1].wait_recv())
    fill2(r1b, b2b, r2b)
    for k in range(1, nx):
        copy2(1, b2b, r2b, k)[0].start()
    grads(text, 0, tg_out)
    done[0].start()
    grads(img, tok, ig_out)
    done[1].start()
    kv_text = reduced(0)
    for j in range(pieces):
        copy_x(j, 2)[0].wait_send()
        copy_sib(j)[0].wait_send()
    for k in range(1, nx):
        copy2(0, b2a, r2a, k)[0].wait_send()
    for k in range(1, ny):
        for part in range(2):
            copy_y(part, k)[0].wait_send()
            copy_rs(0, part, k).wait_send()
            copy_rs(1, part, k).wait_send()
            copy_sum(part, k).wait_send()

    def sent1(k):
        copy1(1, b1b, r1b, k)[0].wait_send()

    loop(1, nseq, sent1)

    for k in range(1, nx):
        copy2(1, b2b, r2b, k)[1].wait_recv()
    got = take(pos_tok, r2b)
    kv_out[...] = jnp.where(own_tok >= 0.0, got, kv_text.astype(F32)).astype(BF16)
    done[2].start()
    for d in done:
        d.wait()
    for k in range(1, nx):
        copy2(1, b2b, r2b, k)[0].wait_send()


def flush(a, b, c, out_a, out_b, out_c, via_a, via_b, via_c, sem):
    ways = ((b, via_b, out_b), (c, via_c, out_c), (a, via_a, out_a))
    into = [pltpu.make_async_copy(p, v, sem.at[0, i]) for i, (p, v, _) in enumerate(ways)]
    away = [pltpu.make_async_copy(v, q, sem.at[1, i]) for i, (_, v, q) in enumerate(ways)]
    for p in into:
        p.start()
    for p, q in zip(into, away):
        p.wait()
        q.start()
    for q in away:
        q.wait()


def per_device(text_embed, image_rows, token_source, slot_dest, norm_gain, kv_weight, kv_cot):
    nx, nseq, ny = lax.axis_size("sec"), lax.axis_size("seq"), lax.axis_size("tp")
    nz = nseq // 2
    tok, feat = text_embed.shape
    slots = image_rows.shape[0]
    rows = tok + slots
    cols = kv_cot.shape[1]
    dma = pltpu.SemaphoreType.DMA
    blk = (2 * nx * cols) // LANES
    exch = [
        pltpu.VMEM((nseq, blk, LANES), BF16),
        pltpu.VMEM((nseq, blk, LANES), BF16),
        pltpu.VMEM((nx, 2 * nseq, cols), BF16),
        pltpu.VMEM((nx, 2 * nseq, cols), BF16),
    ]
    hbm = pl.BlockSpec(memory_space=pl.ANY)
    outs = pl.pallas_call(
        functools.partial(kernel, nx, nz, ny),
        out_shape=(
            jax.ShapeDtypeStruct((tok, cols), BF16),
            jax.ShapeDtypeStruct((tok, feat), BF16),
            jax.ShapeDtypeStruct((slots, feat), BF16),
        ),
        in_specs=[pl.BlockSpec(memory_space=pl.ANY)] * 7,
        out_specs=(hbm, hbm, hbm),
        scratch_shapes=[
            pltpu.VMEM((tok, cols), BF16),
            pltpu.VMEM((tok, feat), BF16),
            pltpu.VMEM((slots, feat), BF16),
            pltpu.VMEM((tok, feat), BF16),
            pltpu.VMEM((slots, feat), BF16),
            pltpu.VMEM((1, tok), jnp.int32),
            pltpu.VMEM((1, slots), jnp.int32),
            pltpu.VMEM((1, feat), F32),
            pltpu.VMEM((8, feat), BF16),
            pltpu.VMEM((tok, cols), BF16),
            pltpu.VMEM((nx, nz, 2, 16, feat // 2), BF16),
            pltpu.VMEM((rows, feat), BF16),
            pltpu.VMEM((ny, rows, cols), BF16),
            pltpu.VMEM((rows, LANES), F32),
            pltpu.VMEM((rows, feat), F32),
            pltpu.VMEM((2, ny, rows, LANES), F32),
            pltpu.VMEM((rows, cols), F32),
            pltpu.VMEM((2, ny, rows, LANES), BF16),
            pltpu.VMEM((2, ny, rows, LANES), BF16),
            pltpu.VMEM((2, 8, rows), F32),
            pltpu.VMEM((2, ny, 8, rows), F32),
            *exch,
            *exch,
            dma((3,)),
            dma((7,)),
            *[dma((3,))] * 2,
            *[dma((4, 3))] * 2,
            *[dma((2,))] * 2,
            *[dma((nz, 3))] * 2,
            *[dma((nz,))] * 2,
            *[dma((2, nseq))] * 2,
            *[dma((2, nx))] * 2,
            *[dma((2, ny))] * 2,
            *[dma((2, 2, ny))] * 2,
            *[dma((2, ny))] * 2,
        ],
        compiler_params=pltpu.CompilerParams(
            collective_id=0, has_side_effects=True, vmem_limit_bytes=58 * 2**20
        ),
        cost_estimate=pl.CostEstimate(
            flops=4 * rows * feat * cols * ny, bytes_accessed=8 * rows * feat, transcendentals=0
        ),
    )(
        text_embed,
        image_rows,
        token_source.reshape(1, tok),
        slot_dest.reshape(1, slots),
        norm_gain.reshape(1, feat),
        kv_weight,
        kv_cot,
    )
    where = pl.BlockSpec(memory_space=pl.ANY)
    return pl.pallas_call(
        flush,
        out_shape=tuple(jax.ShapeDtypeStruct(o.shape, o.dtype) for o in outs),
        in_specs=[where] * 3,
        out_specs=(where,) * 3,
        scratch_shapes=[*[pltpu.VMEM(o.shape, o.dtype) for o in outs], dma((2, 3))],
        compiler_params=pltpu.CompilerParams(vmem_limit_bytes=58 * 2**20),
    )(*outs)


def solution(mesh):
    both = P(("sec", "seq"), "tp")
    rows = P(("sec", "seq"))
    return jax.shard_map(
        per_device,
        mesh=mesh,
        in_specs=(both, both, rows, rows, P("tp"), both, both),
        out_specs=(both, both, both),
        check_vma=False,
    )
```
